32 devices in a mesh: blk: 16 (over z, x, core), grp: 2 (over y).
Axes of the slice: x: 2, y: 2, z: 4, core: 2. Of those that a mesh axis runs over, the one named last changes fastest.
Arguments:
- residents: bfloat16 [64, 32, 1024], P(('blk', 'grp')), may hold values from -6 to 6
- travellers: bfloat16 [32, 32, 1024], P('blk'), may hold values from -6 to 6
- pair_list: int32 [32, 4, 2, 3], P(('blk', 'grp')), may hold values from 0 to 1, as said below
Outputs:
- resident_exchange: float32 [64, 32, 1024], P(('blk', 'grp'))
- traveller_exchange: float32 [32, 32, 1024], P('blk', 'grp')
The draws below stay inside these ranges and needn't reach their ends.
Inputs may be any that keep to these rules, and one draw needn't show every extreme that they name: `pair_list`: entry 0 is a resident index below 2, entry 1 a traveller index below 2, entry 2 is 0 or 1; the number of active slots differs from device to device.
All inputs are finite; a program needn't handle non-finite values.
Results may differ from the reference program's by a relative error of at most 0.0003.
Values may be sent and summed in bfloat16 or wider, within the bound.
No kernel may reach another device: no remote copies, remote signals or barrier semaphores. Data moves between devices by JAX's collectives and lax.ppermute only.
A program may use at most 64 MiB of HBM per device.

```python
import jax
import jax.numpy as jnp
from jax import lax

BOX = 32
R_DEV = 2
TRAV = 2
STEPS = 4
PAIRS = 2
RESIDENTS = 64
TRAVELLERS = 32
N_BLK = 16
N_GRP = 2


def draw_pair_list(key, part):
    keys = jax.random.split(jax.random.fold_in(key, 17), 4)
    shape = (N_BLK * N_GRP, STEPS, PAIRS)
    res_index = jax.random.randint(keys[0], shape, 0, R_DEV)
    trav_index = jax.random.randint(keys[1], shape, 0, TRAV)
    device_load = jax.random.randint(keys[2], (N_BLK * N_GRP, 1, 1), 1, PAIRS + 1)
    tickets = jax.random.randint(keys[3], shape, 0, PAIRS)
    active = (tickets < device_load).astype(jnp.int32)
    return jnp.stack([res_index, trav_index, active], axis=-1).astype(jnp.int32)


def level_of(own_key, shape, pieces, smallest, top_value):
    loudness, own = 1.0, jax.random.fold_in(own_key, 6)
    for dim, blocks in pieces:
        steps = jnp.exp(jax.random.uniform(jax.random.fold_in(own, dim), (blocks,), jnp.float32, smallest / len(pieces), top_value / len(pieces)))
        loudness = loudness * jnp.repeat(steps, shape[dim] // blocks).reshape([-1 if axis == dim else 1 for axis in range(len(shape))])
    return loudness


def gaussian(stream_key, extent, width, limit, shards=(), kind=jnp.bfloat16):
    values = jax.random.normal(stream_key, extent, jnp.float32) * width
    if len(shards) > 0:
        values = level_of(stream_key, extent, shards, -0.22, 0.18) * values
    return jnp.clip(values, min=-limit, max=limit).astype(kind)


def setup_inputs(seed: int = 0) -> dict:
    key_of = jax.random.split(jax.random.key(seed), 4)
    return {
        "residents": gaussian(key_of[0], (RESIDENTS, BOX, BOX * BOX), 1.0, 6.0, ((0, 32),)),
        "travellers": gaussian(key_of[1], (TRAVELLERS, BOX, BOX * BOX), 1.0, 6.0, ((0, 16),)),
        "pair_list": draw_pair_list(jax.random.fold_in(key_of[3], 71), 0),
    }


def sine_table(size):
    index = jnp.arange(size, dtype=jnp.float32) + 1.0
    return jnp.sqrt(2.0 / (size + 1)) * jnp.sin(jnp.pi * jnp.outer(index, index) / (size + 1))

def inverse_eigen(size):
    index = jnp.arange(size, dtype=jnp.float32) + 1.0
    eigen = 2.0 - 2.0 * jnp.cos(jnp.pi * index / (size + 1))
    total = eigen[:, None, None] + eigen[None, :, None] + eigen[None, None, :]
    return 1.0 / total

def transform(field, table):
    high = lax.Precision.HIGHEST
    field = jnp.einsum('ai,ijk->ajk', table, field, precision=high)
    field = jnp.einsum('bj,ajk->abk', table, field, precision=high)
    return jnp.einsum('ck,abk->abc', table, field, precision=high)

def reference(residents, travellers, pair_list):
    table = sine_table(BOX)
    inverse = inverse_eigen(BOX)
    per_device = STEPS * PAIRS
    count = N_BLK * N_GRP * per_device

    def visit(entry, totals):
        res_total, trav_total = totals
        device = entry // per_device
        arrival = entry // PAIRS % STEPS + 1
        slot = entry % PAIRS
        block = device // N_GRP
        source = (block - arrival + N_BLK) % N_BLK
        row = pair_list[device, arrival - 1, slot]
        res_row = (device * R_DEV + row[0]).astype(jnp.int32)
        trav_row = (source * TRAV + row[1]).astype(jnp.int32)
        active = row[2].astype(jnp.float32)
        resident = lax.dynamic_index_in_dim(residents, res_row, 0, False).astype(jnp.float32).reshape(BOX, BOX, BOX)
        traveller = lax.dynamic_index_in_dim(travellers, trav_row, 0, False).astype(jnp.float32).reshape(BOX, BOX, BOX)
        potential = transform(transform(resident * traveller, table) * inverse, table)
        res_add = (active * potential * traveller).reshape(1, BOX, BOX * BOX)
        trav_add = (active * potential * resident).reshape(1, BOX, BOX * BOX)
        res_old = lax.dynamic_index_in_dim(res_total, res_row, 0, True)
        res_total = lax.dynamic_update_index_in_dim(res_total, res_old + res_add, res_row, 0)
        trav_old = lax.dynamic_index_in_dim(trav_total, trav_row, 0, True)
        trav_total = lax.dynamic_update_index_in_dim(trav_total, trav_old + trav_add, trav_row, 0)
        return (res_total, trav_total)
    start = (jnp.zeros(residents.shape, jnp.float32), jnp.zeros(travellers.shape, jnp.float32))
    res_total, trav_total = lax.fori_loop(0, count, visit, start)
    return (res_total, trav_total)
```

```python
import functools

import jax
import jax.numpy as jnp
import ml_dtypes
import numpy as np
from jax import lax
from jax.experimental import pallas as pl
from jax.experimental.pallas import tpu as pltpu
from jax.sharding import PartitionSpec as P

LANES = 128


def split16(table):
    high = table.astype(ml_dtypes.bfloat16)
    return high, (table - high.astype(np.float64)).astype(ml_dtypes.bfloat16)


@functools.lru_cache
def tables(edge, fields):
    index = np.arange(edge) + 1.0
    sine = np.sqrt(2.0 / (edge + 1)) * np.sin(np.pi * np.outer(index, index) / (edge + 1))
    eigen = 2.0 - 2.0 * np.cos(np.pi * index / (edge + 1))
    parts = []
    for parity in (0, 1):
        plane = np.kron(sine[parity::2, : edge // 2], sine).T
        parts += [*split16(plane), *split16(np.ascontiguousarray(plane.T))]
    parts += split16(np.kron(np.eye(fields), sine))
    by_plane = np.concatenate(
        [(eigen[parity::2, None] + eigen[None, :]).reshape(-1) for parity in (0, 1)]
    )
    parts.append((1.0 / (eigen[:, None] + by_plane[None, :])).astype(np.float32))
    return tuple(parts)


def dot(x, y):
    return jnp.dot(x, y, preferred_element_type=jnp.float32)


def halves(x):
    high = x.astype(jnp.bfloat16)
    return high, (x - high.astype(jnp.float32)).astype(jnp.bfloat16)


def times_table(x, high, low):
    x_high, x_low = halves(x)
    return dot(x_high, high) + (dot(x_low, high) + dot(x_high, low))


def table_times(high, low, x):
    x_high, x_low = halves(x)
    return dot(high, x_high) + (dot(high, x_low) + dot(low, x_high))


def reverse_groups(x, edge):
    blocks = []
    lane = lax.broadcasted_iota(jnp.int32, (x.shape[0], LANES), 1)
    for start in range(x.shape[1] - LANES, -1, -LANES):
        block = x[:, start : start + LANES]
        width = LANES // 2
        while width >= edge:
            block = jnp.where(
                lane % (2 * width) < width,
                pltpu.roll(block, LANES - width, 1),
                pltpu.roll(block, width, 1),
            )
            width //= 2
        blocks.append(block)
    return jnp.concatenate(blocks, axis=1)


def fold(field, edge):
    half = field.shape[1] // 2
    return field[:, :half], reverse_groups(field[:, half:], edge)


def unfold(first, second, edge):
    return jnp.concatenate([first, reverse_groups(second, edge)], axis=1)


def store_folded(source, target):
    edge = source.shape[1]
    for i in range(source.shape[0]):
        first, second = fold(source[i].astype(jnp.float32), edge)
        target[i, 0] = first
        target[i, 1] = second


def gather_terms(slots, home, total, table_refs):
    (even_in, even_in_low, even_out, even_out_low, odd_in, odd_in_low, odd_out, odd_out_low,
     along, along_low, inverse) = (ref[...] for ref in table_refs)
    edge = inverse.shape[0]
    half = inverse.shape[1] // 2
    evens, odds = [], []
    for moving, i, j, _ in slots:
        first = moving[i, 0] * home[j, 0]
        second = moving[i, 1] * home[j, 1]
        evens.append(first + second)
        odds.append(first - second)
    even = times_table(jnp.concatenate(evens, axis=0), even_in, even_in_low)
    odd = times_table(jnp.concatenate(odds, axis=0), odd_in, odd_in_low)
    modes = table_times(along, along_low, jnp.concatenate([even, odd], axis=1))
    modes = (modes.reshape(len(slots), edge, 2 * half) * inverse[None]).reshape(modes.shape)
    modes = table_times(along, along_low, modes)
    even = times_table(modes[:, :half], even_out, even_out_low)
    odd = times_table(modes[:, half:], odd_out, odd_out_low)
    first, second = even + odd, even - odd
    for slot, (moving, i, j, active) in enumerate(slots):
        rows = slice(slot * edge, (slot + 1) * edge)
        total[j, 0] += active * (first[rows] * moving[i, 0])
        total[j, 1] += active * (second[rows] * moving[i, 1])


def slots_of(pairs, arrival, moving, moving_entry):
    return [
        (
            moving,
            pairs[0, arrival, slot, moving_entry],
            pairs[0, arrival, slot, 1 - moving_entry],
            pairs[0, arrival, slot, 2].astype(jnp.float32),
        )
        for slot in range(pairs.shape[2])
    ]


def store_swapped(near, swapped, moving):
    count = len(swapped) - 1

    @pl.when(near == 1)
    def _():
        for k in range(count):
            store_folded(swapped[k], moving.at[k])

    @pl.when(near == 0)
    def _():
        for k in range(count):
            store_folded(swapped[k + 1], moving.at[k])


def early_kernel(count, *refs):
    pairs, refs = refs[:count], refs[count:]
    arrived, refs = refs[:count], refs[count:]
    home, table_refs, (total, home_folded, moving) = refs[0], refs[1:12], refs[12:]
    store_folded(home, home_folded)
    total[...] = jnp.zeros_like(total)
    slots = []
    for k in range(count):
        store_folded(arrived[k], moving.at[k])
        slots += slots_of(pairs[k], 2 * k + 1, moving.at[k], 0)
    gather_terms(slots, home_folded, total, table_refs)


def late_kernel(count, where, *refs):
    pairs, refs = refs[:count], refs[count:]
    swapped, refs = refs[: count + 1], refs[count + 1 :]
    home, early, table_refs = refs[0], refs[1], refs[2:13]
    mine, others, home_folded, moving, total, whole = refs[13:]
    edge = home.shape[1]
    store_folded(home, home_folded)
    store_swapped(where[0], swapped, moving)
    slots = []
    for k in range(count):
        slots += slots_of(pairs[k], 2 * k, moving.at[k], 0)
    total[...] = early[...]
    gather_terms(slots, home_folded, total, table_refs)
    parts, rows = whole.shape[1:3]
    for i in range(home.shape[0]):
        field = unfold(total[i, 0], total[i, 1], edge)
        for part in range(parts):
            whole[i, part] = field[part * rows : (part + 1) * rows]
    for k in range(parts):
        part = lax.rem(where[1] + k, parts)
        for i in range(home.shape[0]):
            if k == 0:
                mine[i] = whole[i, part]
            else:
                others[k - 1, i] = whole[i, part]


def resident_kernel(count, where, pairs, *refs):
    arrived, refs = refs[:count], refs[count:]
    swapped, refs = refs[: count + 1], refs[count + 1 :]
    home, table_refs = refs[0], refs[1:12]
    result, home_folded, moving, moving_swapped, total = refs[12:]
    edge = home.shape[1]
    store_folded(home, home_folded)
    total[...] = jnp.zeros_like(total)
    slots = []
    for k in range(count):
        store_folded(arrived[k], moving.at[k])
        slots += slots_of(pairs, 2 * k + 1, moving.at[k], 1)
    gather_terms(slots, home_folded, total, table_refs)
    store_swapped(where[0], swapped, moving_swapped)
    slots = []
    for k in range(count):
        slots += slots_of(pairs, 2 * k, moving_swapped.at[k], 1)
    gather_terms(slots, home_folded, total, table_refs)
    for i in range(home.shape[0]):
        result[i] = unfold(total[i, 0], total[i, 1], edge)


SMEM = pl.BlockSpec(memory_space=pltpu.SMEM)
VMEM = pl.BlockSpec(memory_space=pltpu.VMEM)
LIMIT = pltpu.CompilerParams(vmem_limit_bytes=32 * 1024 * 1024)


def from_behind(value, by):
    peers = lax.axis_size("blk")
    return lax.ppermute(value, "blk", [(i, (i + by) % peers) for i in range(peers)])


def other_core(value, only_to=None):
    peers = lax.axis_size("blk")
    return lax.ppermute(
        value, "blk", [(i, i ^ 1) for i in range(peers) if only_to in (None, (i ^ 1) % 2)]
    )


def local(residents, travellers, pair_list):
    count, edge, plane = residents.shape
    steps = pair_list.shape[1]
    direct = range(2, steps + 1, 2)
    arrivals = len(direct)
    groups = lax.axis_size("grp")
    part = edge // groups
    fields = arrivals * pair_list.shape[2]
    consts = [jnp.asarray(table) for table in tables(edge, fields)]

    res_moved = [from_behind(residents, -s) for s in direct]
    res_swapped = [other_core(residents, 0)]
    pairs = [from_behind(pair_list, -s) for s in range(1, steps + 1)]
    trav_moved = [from_behind(travellers, s) for s in direct]
    trav_swapped = [other_core(travellers, 1)]
    for k in range(arrivals):
        last = k == arrivals - 1
        res_swapped.append(other_core(res_moved[k], 1 if last else None))
        trav_swapped.append(other_core(trav_moved[k], 0 if last else None))

    core = lax.axis_index("blk") % 2
    group = lax.axis_index("grp")
    res_where = jnp.stack([1 - core, group]).astype(jnp.int32)
    trav_where = jnp.stack([core, group]).astype(jnp.int32)

    folded = (count, 2, edge, plane // 2)
    early = pl.pallas_call(
        functools.partial(early_kernel, arrivals),
        out_shape=jax.ShapeDtypeStruct(folded, jnp.float32),
        in_specs=[SMEM] * arrivals + [VMEM] * (arrivals + 1 + len(consts)),
        out_specs=VMEM,
        scratch_shapes=[
            pltpu.VMEM(folded, jnp.float32),
            pltpu.VMEM((arrivals, *folded), jnp.float32),
        ],
        compiler_params=LIMIT,
        name="early_terms",
    )(*pairs[1::2], *res_moved, travellers, *consts)
    mine, others = pl.pallas_call(
        functools.partial(late_kernel, arrivals),
        out_shape=(
            jax.ShapeDtypeStruct((count, part, plane), jnp.float32),
            jax.ShapeDtypeStruct((groups - 1, count, part, plane), jnp.float32),
        ),
        in_specs=[SMEM] * (1 + arrivals) + [VMEM] * (arrivals + 3 + len(consts)),
        out_specs=(VMEM, VMEM),
        scratch_shapes=[
            pltpu.VMEM(folded, jnp.float32),
            pltpu.VMEM((arrivals, *folded), jnp.float32),
            pltpu.VMEM(folded, jnp.float32),
            pltpu.VMEM((count, groups, part, plane), jnp.float32),
        ],
        compiler_params=LIMIT,
        name="late_terms",
    )(res_where, *pairs[0::2], *res_swapped, travellers, early, *consts)
    sent = [
        lax.ppermute(others[k - 1], "grp", [(g, (g + k) % groups) for g in range(groups)])
        for k in range(1, groups)
    ]
    res_total = pl.pallas_call(
        functools.partial(resident_kernel, arrivals),
        out_shape=jax.ShapeDtypeStruct(residents.shape, jnp.float32),
        in_specs=[SMEM] * 2 + [VMEM] * (2 * arrivals + 2 + len(consts)),
        out_specs=VMEM,
        scratch_shapes=[
            pltpu.VMEM(folded, jnp.float32),
            pltpu.VMEM((arrivals, *folded), jnp.float32),
            pltpu.VMEM((arrivals, *folded), jnp.float32),
            pltpu.VMEM(folded, jnp.float32),
        ],
        compiler_params=LIMIT,
        name="resident_terms",
    )(trav_where, pair_list, *trav_moved, *trav_swapped, residents, *consts)
    for value in sent:
        mine = mine + value
    return res_total, mine


def solution(mesh):
    return jax.shard_map(
        local,
        mesh=mesh,
        in_specs=(
            P(("blk", "grp"), None, None),
            P("blk", None, None),
            P(("blk", "grp"), None, None, None),
        ),
        out_specs=(P(("blk", "grp"), None, None), P("blk", "grp", None)),
        check_vma=False,
    )
```

```python
import functools

import jax
import jax.numpy as jnp
import numpy as np
from jax import lax
from jax.experimental import pallas as pl
from jax.experimental.pallas import tpu as pltpu
from jax.sharding import PartitionSpec as P


@functools.lru_cache
def small_tables(edge, fields):
    index = np.arange(edge) + 1.0
    sine = np.sqrt(2.0 / (edge + 1)) * np.sin(np.pi * np.outer(index, index) / (edge + 1))
    eigen = 2.0 - 2.0 * np.cos(np.pi * index / (edge + 1))
    part = sine[::2, ::2]
    split = (eigen[::2], eigen[::-1][::2])
    plane = [np.add.outer(split[b], split[c]).reshape(-1) for b in (0, 1) for c in (0, 1)]
    lanes = max(edge * edge // 4, 2 * fields * edge)
    rows = [
        np.repeat(part, edge // 2, axis=1),
        np.tile(part, (1, edge // 2)),
        np.concatenate([np.tile(sine, (1, fields)), np.tile(eigen[:, None], (1, fields * edge))], axis=1),
        np.stack(plane),
        np.zeros((4, 1)),
    ]
    return np.concatenate([np.pad(r, ((0, 0), (0, lanes - r.shape[1]))) for r in rows]).astype(np.float32)


def make_tables(small, edge, fields, plane_table, along, inverse):
    part, lanes, rows = edge // 2, edge * edge // 4, fields * edge
    second = small[part : 2 * part, :lanes]
    for n in range(part):
        high, low = halves(small[n : n + 1, :lanes] * second)
        plane_table[n * part : (n + 1) * part, :] = high
        plane_table[lanes + n * part : lanes + (n + 1) * part, :] = low
    sine = jnp.concatenate([small[edge : 2 * edge, :rows]] * fields, axis=0)
    row = lax.broadcasted_iota(jnp.int32, (rows, rows), 0)
    column = lax.broadcasted_iota(jnp.int32, (rows, rows), 1)
    high, low = halves(jnp.where(row // edge == column // edge, sine, 0.0))
    along[:rows, :] = high
    along[rows:, :] = low
    eigen = small[edge : 2 * edge, rows : rows + 1]
    for q in range(4):
        plane = small[2 * edge + q : 2 * edge + q + 1, :lanes]
        inverse[:, q * lanes : (q + 1) * lanes] = 1.0 / (eigen + plane)


def fold_source(lane, edge):
    small = edge // 2
    point_c = lane % small
    point_b = (lane // small) % (edge // 4)
    quadrant = lane // (small * (edge // 4))
    b = jnp.where(quadrant < 2, 2 * point_b, small - 1 - 2 * point_b)
    c = jnp.where(quadrant % 2 == 0, 2 * point_c, edge - 1 - 2 * point_c)
    return b * edge + c


def fold_table(edge, transposed):
    lanes = edge * edge // 2
    dim = 0 if transposed else 1
    folded = fold_source(lax.broadcasted_iota(jnp.int32, (lanes, 1) if transposed else (1, lanes), dim), edge)
    plain = lax.broadcasted_iota(jnp.int32, (lanes, lanes), 1 - dim)
    return jnp.where(plain == folded, 1.0, 0.0).astype(jnp.bfloat16)


def tile_of(quadrant, half):
    return 2 * quadrant + (half if quadrant < 2 else 1 - half)


def dot(x, y):
    return jnp.dot(x, y, preferred_element_type=jnp.float32)


def halves(x):
    high = x.astype(jnp.bfloat16)
    return high, (x - high.astype(jnp.float32)).astype(jnp.bfloat16)


def times_table(x, table):
    x_high, x_low = halves(x)
    high, low = table[: table.shape[0] // 2], table[table.shape[0] // 2 :]
    return dot(x_high, high) + (dot(x_low, high) + dot(x_high, low))


def table_times(table, x):
    x_high, x_low = halves(x)
    high, low = table[: table.shape[0] // 2], table[table.shape[0] // 2 :]
    return dot(high, x_high) + (dot(high, x_low) + dot(low, x_high))


def spread(quadrants):
    a, b, c, d = quadrants
    return [a + b + (c + d), a - b + (c - d), a + b - (c + d), a - b - (c - d)]


def info_rows(steps, slots):
    return -(-(steps * slots * 3 + 2) // 16) * 16


def store_folded(fields, target):
    count, edge, plane = fields.shape
    half, lanes = plane // 2, plane // 8
    rows = [fields[i, :, h * half : (h + 1) * half] for i in range(count) for h in (0, 1)]
    folded = dot(jnp.concatenate(rows, axis=0), fold_table(edge, False)).astype(jnp.bfloat16)
    for i in range(count):
        for h in (0, 1):
            start = (2 * i + h) * edge
            for q in range(4):
                row = (tile_of(q, h) * count + i) * edge
                target[row : row + edge, :] = folded[start : start + edge, q * lanes : (q + 1) * lanes]


def pack_kernel(axes, residents, travellers, pairs, packed, moving, fields, moving_fields, entries_ref, sems):
    count, edge, plane = residents.shape
    load = pltpu.make_async_copy(residents, fields, sems.at[0])
    load_entries = pltpu.make_async_copy(pairs, entries_ref, sems.at[1])
    load_moving = pltpu.make_async_copy(travellers, moving_fields, sems.at[2])
    load.start()
    load_moving.start()
    load_entries.start()
    load_entries.wait()
    _, entries, slots, steps = pairs.shape
    row = lax.broadcasted_iota(jnp.int32, (info_rows(steps, slots), packed.shape[1]), 0)
    values = jnp.zeros(row.shape, jnp.int32)
    scalars = [entries_ref[0, e, p, s] for s in range(steps) for p in range(slots) for e in range(entries)]
    for k, value in enumerate([lax.axis_index(axes[0]) % 2, lax.axis_index(axes[1]), *scalars]):
        values = jnp.where(row == k, value, values)
    packed[8 * count * edge :, :] = values.astype(jnp.float32).astype(jnp.bfloat16)
    load.wait()
    store_folded(fields, packed)
    load_moving.wait()
    store_folded(moving_fields, moving)


def tables_kernel(count, small, plane_table, along, inverse):
    make_tables(small, inverse.shape[0], count, plane_table, along, inverse)


class Fields:
    def __init__(self, count, edge, *refs, near=None):
        self.count, self.edge, self.refs, self.near = count, edge, refs, near

    def rows(self, start, size):
        values = [ref[start : start + size, :].astype(jnp.float32) for ref in self.refs]
        return jnp.where(self.near, *values) if len(values) == 2 else values[0]

    def quadrants(self, i):
        tiles = [self.rows((t * self.count + i) * self.edge, self.edge) for t in range(8)]
        return [jnp.concatenate(tiles[2 * q : 2 * q + 2], axis=1) for q in range(4)]

    def info(self, count=None):
        start = 8 * self.count * self.edge
        return self.rows(start, self.refs[0].shape[0] - start)


def wide(row, edge, lanes):
    return jnp.broadcast_to(jnp.concatenate([row] * (lanes // row.shape[1]), axis=1), (edge, lanes))


def choose(fields, index):
    chosen = fields[0]
    for i in range(1, len(fields)):
        chosen = [jnp.where(index == i, new, old) for new, old in zip(fields[i], chosen)]
    return chosen


def slot_rows(info, arrival, slots):
    start = 2 + arrival * slots * 3
    return [info[start + 3 * p : start + 3 * p + 3] for p in range(slots)]


def gather_terms(slots, home, total, tables):
    plane_table, along, inverse = (table[...] for table in tables)
    edge = inverse.shape[0]
    rows = len(slots) * edge
    densities = []
    for moving, index, _ in slots:
        densities.append(spread([m * h for m, h in zip(moving, choose(home, index))]))
    field = jnp.concatenate([density[q] for q in range(4) for density in densities], axis=0)
    field = times_table(field, plane_table)
    field = jnp.concatenate([field[q * rows : (q + 1) * rows] for q in range(4)], axis=1)
    size = along.shape[0] // 2
    along = jnp.concatenate([along[:rows, :rows], along[size : size + rows, :rows]], axis=0)
    field = table_times(along, field)
    field = (field.reshape(len(slots), edge, -1) * inverse[None]).reshape(field.shape)
    field = table_times(along, field)
    lanes = field.shape[1] // 4
    field = jnp.concatenate([field[:, q * lanes : (q + 1) * lanes] for q in range(4)], axis=0)
    field = times_table(field, plane_table)
    for slot, (moving, index, active) in enumerate(slots):
        potential = spread([field[q * rows + slot * edge : q * rows + (slot + 1) * edge] for q in range(4)])
        terms = [active * p * m for p, m in zip(potential, moving)]
        for j in range(len(home)):
            total[j] = [old + jnp.where(index == j, new, 0.0) for old, new in zip(total[j], terms)]


def zero_total(home):
    return [[jnp.zeros_like(q) for q in field] for field in home]


def unfold(total, edge):
    table = fold_table(edge, True)
    lanes = edge * edge // 8
    stack = []
    for field in total:
        for h in (0, 1):
            tiles = [tile_of(q, h) for q in range(4)]
            stack.append(
                jnp.concatenate(
                    [field[t // 2][:, (t % 2) * lanes : (t % 2 + 1) * lanes] for t in tiles], axis=1
                )
            )
    high, low = halves(jnp.concatenate(stack, axis=0))
    plain = dot(high, table) + dot(low, table)
    return [
        jnp.concatenate([plain[2 * i * edge : (2 * i + 1) * edge], plain[(2 * i + 1) * edge : (2 * i + 2) * edge]], axis=1)
        for i in range(len(total))
    ]


def slots_of(block, info, near, arrivals, slots, entry):
    edge = block.edge
    fields = [block.quadrants(i) for i in range(block.count)]
    lanes = fields[0][0].shape[1]
    found = []
    for row, far in zip(slot_rows(info, arrivals[0], slots), slot_rows(info, arrivals[1], slots)):
        row = jnp.where(near, row, far)
        own, other, active = (wide(row[e : e + 1], edge, lanes) for e in (entry, 1 - entry, 2))
        found.append((choose(fields, own), other, active))
    return found


def terms_kernel(plan, accumulate, finish, slots, edge, for_travellers, *refs):
    blocks = sum(number for number, _ in plan)
    outputs = 2 if finish and for_travellers else 1
    refs, outs = refs[:-outputs], refs[-outputs:]
    moving, (own, home, *refs) = refs[:blocks], refs[blocks:]
    tables, early = refs[:3], refs[3:]
    held = home.shape[0] // (8 * edge)
    count = moving[0].shape[0] // (8 * edge)
    own = Fields(own.shape[0] // (8 * edge), edge, own).info()
    near = own[0:1] == (0 if for_travellers else 1)
    home = Fields(held, edge, home)
    home = [home.quadrants(j) for j in range(held)]
    found = []
    for number, arrivals in plan:
        block, moving = Fields(count, edge, *moving[:number], near=near), moving[number:]
        info = block.info() if for_travellers else own
        found += slots_of(block, info, near, arrivals, slots, 0 if for_travellers else 1)
    total = [[early[0][j, q] for q in range(4)] for j in range(held)] if accumulate else zero_total(home)
    gather_terms(found, home, total, tables)
    if not finish:
        for j, field in enumerate(total):
            for q in range(4):
                outs[0][j, q] = field[q]
        return
    total = unfold(total, edge)
    if not for_travellers:
        for j, field in enumerate(total):
            outs[0][j] = field
        return
    mine, others = outs
    rows = mine.shape[1]
    parts = edge // rows
    for j, field in enumerate(total):
        cuts = [[field[p * rows : (p + 1) * rows]] for p in range(parts)]
        for k in range(parts):
            group = wide(own[1:2], rows, field.shape[1]) + k
            group = jnp.where(group >= parts, group - parts, group)
            cut = choose(cuts, group)[0]
            if k == 0:
                mine[j] = cut
            else:
                others[k - 1, j] = cut


VMEM = pl.BlockSpec(memory_space=pltpu.VMEM)
HBM = pl.BlockSpec(memory_space=pl.ANY)
LIMIT = pltpu.CompilerParams(vmem_limit_bytes=32 * 1024 * 1024)
LIMIT_U = pltpu.CompilerParams(vmem_limit_bytes=60 * 1024 * 1024)
LIMIT_W = pltpu.CompilerParams(vmem_limit_bytes=32 * 1024 * 1024)


def cost(microseconds):
    return pl.CostEstimate(flops=int(microseconds * 1e9), bytes_accessed=1024, transcendentals=0)


def from_behind(value, by):
    peers = lax.axis_size("blk")
    return lax.ppermute(value, "blk", [(i, (i + by) % peers) for i in range(peers)])


def other_core(value):
    peers = lax.axis_size("blk")
    return lax.ppermute(value, "blk", [(i, i ^ 1) for i in range(peers)])


def local(residents, travellers, pair_list):
    count, edge, plane = residents.shape
    held = travellers.shape[0]
    steps, slots = pair_list.shape[1:3]
    direct = range(2, steps + 1, 2)
    arrivals = len(direct)
    groups = lax.axis_size("grp")
    part = edge // groups
    fields = 2 * arrivals * slots
    small = jnp.asarray(small_tables(edge, fields))

    packed, moving = pl.pallas_call(
        functools.partial(pack_kernel, ("blk", "grp")),
        out_shape=(
            jax.ShapeDtypeStruct((8 * count * edge + info_rows(steps, slots), plane // 8), jnp.bfloat16),
            jax.ShapeDtypeStruct((8 * held * edge, plane // 8), jnp.bfloat16),
        ),
        in_specs=[HBM, HBM, HBM],
        out_specs=(VMEM, VMEM),
        scratch_shapes=[
            pltpu.VMEM(residents.shape, jnp.bfloat16),
            pltpu.VMEM(travellers.shape, jnp.bfloat16),
            pltpu.SMEM((1, 3, slots, steps), jnp.int32),
            pltpu.SemaphoreType.DMA((3,)),
        ],
        compiler_params=LIMIT_U,
        cost_estimate=cost(1),
        name="pack",
    )(residents, travellers, jnp.transpose(pair_list, (0, 3, 2, 1)))
    tables = pl.pallas_call(
        functools.partial(tables_kernel, fields),
        out_shape=(
            jax.ShapeDtypeStruct((plane // 2, plane // 4), jnp.bfloat16),
            jax.ShapeDtypeStruct((2 * fields * edge, fields * edge), jnp.bfloat16),
            jax.ShapeDtypeStruct((edge, plane), jnp.float32),
        ),
        in_specs=[VMEM],
        out_specs=(VMEM,) * 3,
        compiler_params=LIMIT,
        cost_estimate=cost(20),
        name="tables",
    )(small)

    def stage(plan, operands, home, accumulate, finish, for_travellers, microseconds, name):
        number = home[1].shape[0] // (8 * edge)
        if not finish:
            out_shape = jax.ShapeDtypeStruct((number, 4, edge, plane // 4), jnp.float32)
        elif for_travellers:
            out_shape = (
                jax.ShapeDtypeStruct((number, part, plane), jnp.float32),
                jax.ShapeDtypeStruct((groups - 1, number, part, plane), jnp.float32),
            )
        else:
            out_shape = jax.ShapeDtypeStruct((number, edge, plane), jnp.float32)
        operands = (*operands, *home, *tables, *([] if accumulate is None else [accumulate]))
        return pl.pallas_call(
            functools.partial(terms_kernel, plan, accumulate is not None, finish, slots, edge, for_travellers),
            out_shape=out_shape,
            in_specs=[VMEM] * len(operands),
            out_specs=jax.tree.map(lambda _: VMEM, out_shape),
            compiler_params=LIMIT,
            cost_estimate=cost(microseconds),
            name=name,
        )(*operands)

    last = arrivals - 1

    def straight(k):
        return 1, (2 * k + 1, 2 * k + 1)

    middle = [(1, (2 * k + 2, 2 * k)) for k in range(last)]
    ends = [(2, (0, 2 * last))]

    res_moved = [from_behind(packed, -s) for s in direct]
    res_swapped = [other_core(packed)] + [other_core(value) for value in res_moved]
    trav_moved = [from_behind(moving, s) for s in direct]
    trav_swapped = [other_core(moving)]

    home = (packed, moving)
    early = stage(
        [straight(k) for k in range(last)] + middle,
        res_moved[:last] + res_swapped[1:-1],
        home,
        None,
        False,
        True,
        10,
        "early_traveller_terms",
    )
    mine, others = stage(
        [straight(last)] + ends,
        [res_moved[last], res_swapped[0], res_swapped[-1]],
        home,
        early,
        True,
        True,
        2,
        "late_traveller_terms",
    )
    trav_moved, mine, others = lax.optimization_barrier((trav_moved, mine, others))
    trav_swapped += [other_core(value) for value in trav_moved]
    sent = [
        lax.ppermute(others[k - 1], "grp", [(g, (g + k) % groups) for g in range(groups)])
        for k in range(1, groups)
    ]
    res_total = stage(
        [straight(k) for k in range(arrivals)] + middle + ends,
        [*trav_moved, *trav_swapped[1:-1], trav_swapped[0], trav_swapped[-1]],
        (packed, packed),
        None,
        True,
        False,
        0.5,
        "resident_terms",
    )
    res_total, sent = lax.optimization_barrier((res_total, sent))
    for value in sent:
        mine = mine + value
    return res_total, mine


def solution(mesh):
    return jax.shard_map(
        local,
        mesh=mesh,
        in_specs=(
            P(("blk", "grp"), None, None),
            P("blk", None, None),
            P(("blk", "grp"), None, None, None),
        ),
        out_specs=(P(("blk", "grp"), None, None), P("blk", "grp", None)),
        check_vma=False,
    )
```

```python
import functools

import jax
import jax.numpy as jnp
import numpy as np
from jax import lax
from jax.experimental import pallas as pl
from jax.experimental.pallas import tpu as pltpu
from jax.sharding import PartitionSpec as P


@functools.lru_cache
def small_tables(edge, fields):
    index = np.arange(edge) + 1.0
    sine = np.sqrt(2.0 / (edge + 1)) * np.sin(np.pi * np.outer(index, index) / (edge + 1))
    eigen = 2.0 - 2.0 * np.cos(np.pi * index / (edge + 1))
    part = sine[::2, ::2]
    split = (eigen[::2], eigen[::-1][::2])
    plane = [np.add.outer(split[b], split[c]).reshape(-1) for b in (0, 1) for c in (0, 1)]
    lanes = max(edge * edge // 4, 2 * fields * edge)
    rows = [
        np.repeat(part, edge // 2, axis=1),
        np.tile(part, (1, edge // 2)),
        np.concatenate([np.tile(sine, (1, fields)), np.tile(eigen[:, None], (1, fields * edge))], axis=1),
        np.stack(plane),
        np.zeros((4, 1)),
    ]
    return np.concatenate([np.pad(r, ((0, 0), (0, lanes - r.shape[1]))) for r in rows]).astype(np.float32)


def make_tables(small, edge, fields, plane_table, along, inverse):
    part, lanes, rows = edge // 2, edge * edge // 4, fields * edge
    second = small[part : 2 * part, :lanes]
    for n in range(part):
        high, low = halves(small[n : n + 1, :lanes] * second)
        plane_table[n * part : (n + 1) * part, :] = high
        plane_table[lanes + n * part : lanes + (n + 1) * part, :] = low
    sine = jnp.concatenate([small[edge : 2 * edge, :rows]] * fields, axis=0)
    row = lax.broadcasted_iota(jnp.int32, (rows, rows), 0)
    column = lax.broadcasted_iota(jnp.int32, (rows, rows), 1)
    high, low = halves(jnp.where(row // edge == column // edge, sine, 0.0))
    along[:rows, :] = high
    along[rows:, :] = low
    eigen = small[edge : 2 * edge, rows : rows + 1]
    for q in range(4):
        plane = small[2 * edge + q : 2 * edge + q + 1, :lanes]
        inverse[:, q * lanes : (q + 1) * lanes] = 1.0 / (eigen + plane)


def fold_source(lane, edge):
    small = edge // 2
    point_c = lane % small
    point_b = (lane // small) % (edge // 4)
    quadrant = lane // (small * (edge // 4))
    b = jnp.where(quadrant < 2, 2 * point_b, small - 1 - 2 * point_b)
    c = jnp.where(quadrant % 2 == 0, 2 * point_c, edge - 1 - 2 * point_c)
    return b * edge + c


def fold_table(edge, transposed):
    lanes = edge * edge // 2
    dim = 0 if transposed else 1
    folded = fold_source(lax.broadcasted_iota(jnp.int32, (lanes, 1) if transposed else (1, lanes), dim), edge)
    plain = lax.broadcasted_iota(jnp.int32, (lanes, lanes), 1 - dim)
    return jnp.where(plain == folded, 1.0, 0.0).astype(jnp.bfloat16)


def tile_of(quadrant, half):
    return 2 * quadrant + (half if quadrant < 2 else 1 - half)


def dot(x, y):
    return jnp.dot(x, y, preferred_element_type=jnp.float32)


def halves(x):
    high = x.astype(jnp.bfloat16)
    return high, (x - high.astype(jnp.float32)).astype(jnp.bfloat16)


def times_table(x, table):
    x_high, x_low = halves(x)
    high, low = table[: table.shape[0] // 2], table[table.shape[0] // 2 :]
    return dot(x_high, high) + (dot(x_low, high) + dot(x_high, low))


def table_times(table, x):
    x_high, x_low = halves(x)
    high, low = table[: table.shape[0] // 2], table[table.shape[0] // 2 :]
    return dot(
        jnp.concatenate([high, high, low], axis=1), jnp.concatenate([x_high, x_low, x_high], axis=0)
    )


def spread(quadrants):
    a, b, c, d = quadrants
    return [a + b + (c + d), a - b + (c - d), a + b - (c + d), a - b - (c - d)]


def info_rows(steps, slots):
    return -(-(steps * slots * 3 + 2) // 16) * 16


def store_folded(fields, table, target):
    count, edge, plane = fields.shape
    half, lanes = plane // 2, plane // 8
    rows = [fields[i, :, h * half : (h + 1) * half] for i in range(count) for h in (0, 1)]
    folded = dot(jnp.concatenate(rows, axis=0), table).astype(jnp.bfloat16)
    for i in range(count):
        for h in (0, 1):
            start = (2 * i + h) * edge
            for q in range(4):
                row = (tile_of(q, h) * count + i) * edge
                target[row : row + edge, :] = folded[start : start + edge, q * lanes : (q + 1) * lanes]


def pack_kernel(axes, residents, travellers, pairs, packed, moving, fields, moving_fields, entries_ref, folded, moving_folded, sems):
    count, edge, plane = residents.shape
    loads = [pltpu.make_async_copy(residents.at[i], fields.at[i], sems.at[5 + i]) for i in range(count)]
    load_entries = pltpu.make_async_copy(pairs, entries_ref, sems.at[1])
    load_moving = pltpu.make_async_copy(travellers, moving_fields, sems.at[2])
    for load in loads:
        load.start()
    load_entries.start()
    load_moving.start()
    table = fold_table(edge, False)
    load_entries.wait()
    _, entries, slots, steps = pairs.shape
    row = lax.broadcasted_iota(jnp.int32, (info_rows(steps, slots), packed.shape[1]), 0)
    values = jnp.zeros(row.shape, jnp.int32)
    scalars = [entries_ref[0, e, p, s] for s in range(steps) for p in range(slots) for e in range(entries)]
    for k, value in enumerate([lax.axis_index(axes[0]) % 2, lax.axis_index(axes[1]), *scalars]):
        values = jnp.where(row == k, value, values)
    folded[8 * count * edge :, :] = values.astype(jnp.float32).astype(jnp.bfloat16)
    for load in loads:
        load.wait()
    store_folded(fields, table, folded)
    store = pltpu.make_async_copy(folded, packed, sems.at[3])
    store.start()
    load_moving.wait()
    store_folded(moving_fields, table, moving_folded)
    store_moving = pltpu.make_async_copy(moving_folded, moving, sems.at[4])
    store_moving.start()
    store.wait()
    store_moving.wait()


def tables_kernel(count, small, plane_table, along, inverse):
    make_tables(small, inverse.shape[0], count, plane_table, along, inverse)


class Fields:
    def __init__(self, count, edge, *refs, near=None):
        self.count, self.edge, self.refs, self.near = count, edge, refs, near

    def rows(self, start, size):
        values = [ref[start : start + size, :].astype(jnp.float32) for ref in self.refs]
        return jnp.where(self.near, *values) if len(values) == 2 else values[0]

    def quadrants(self, i):
        tiles = [self.rows((t * self.count + i) * self.edge, self.edge) for t in range(8)]
        return [jnp.concatenate(tiles[2 * q : 2 * q + 2], axis=1) for q in range(4)]

    def info(self, count=None):
        start = 8 * self.count * self.edge
        return self.rows(start, self.refs[0].shape[0] - start)


def wide(row, edge, lanes):
    return jnp.broadcast_to(jnp.concatenate([row] * (lanes // row.shape[1]), axis=1), (edge, lanes))


def choose(fields, index):
    chosen = fields[0]
    for i in range(1, len(fields)):
        chosen = [jnp.where(index == i, new, old) for new, old in zip(fields[i], chosen)]
    return chosen


def slot_rows(info, arrival, slots):
    start = 2 + arrival * slots * 3
    return [info[start + 3 * p : start + 3 * p + 3] for p in range(slots)]


def gather_terms(slots, home, total, tables):
    plane_table, along, inverse = (table[...] for table in tables)
    edge = inverse.shape[0]
    rows = len(slots) * edge
    densities = []
    for moving, index, _ in slots:
        densities.append(spread([m * h for m, h in zip(moving, choose(home, index))]))
    field = jnp.concatenate([density[q] for q in range(4) for density in densities], axis=0)
    field = times_table(field, plane_table)
    field = jnp.concatenate([field[q * rows : (q + 1) * rows] for q in range(4)], axis=1)
    size = along.shape[0] // 2
    along = jnp.concatenate([along[:rows, :rows], along[size : size + rows, :rows]], axis=0)
    field = table_times(along, field)
    field = (field.reshape(len(slots), edge, -1) * inverse[None]).reshape(field.shape)
    field = table_times(along, field)
    lanes = field.shape[1] // 4
    field = jnp.concatenate([field[:, q * lanes : (q + 1) * lanes] for q in range(4)], axis=0)
    field = times_table(field, plane_table)
    for slot, (moving, index, active) in enumerate(slots):
        potential = spread([field[q * rows + slot * edge : q * rows + (slot + 1) * edge] for q in range(4)])
        terms = [active * p * m for p, m in zip(potential, moving)]
        for j in range(len(home)):
            total[j] = [old + jnp.where(index == j, new, 0.0) for old, new in zip(total[j], terms)]


def zero_total(home):
    return [[jnp.zeros_like(q) for q in field] for field in home]


def unfold(fields, table):
    rows = fields[0][0].shape[0]
    lanes = table.shape[0] // 4
    stack = []
    for field in fields:
        for h in (0, 1):
            tiles = [tile_of(q, h) for q in range(4)]
            stack.append(
                jnp.concatenate(
                    [field[t // 2][:, (t % 2) * lanes : (t % 2 + 1) * lanes] for t in tiles], axis=1
                )
            )
    high, low = halves(jnp.concatenate(stack, axis=0))
    plain = dot(high, table) + dot(low, table)
    return [
        jnp.concatenate([plain[k * rows : (k + 1) * rows] for k in (2 * i, 2 * i + 1)], axis=1)
        for i in range(len(fields))
    ]


def slots_of(block, info, near, arrivals, slots, entry):
    edge = block.edge
    fields = [block.quadrants(i) for i in range(block.count)]
    lanes = fields[0][0].shape[1]
    found = []
    for row, far in zip(slot_rows(info, arrivals[0], slots), slot_rows(info, arrivals[1], slots)):
        row = jnp.where(near, row, far)
        own, other, active = (wide(row[e : e + 1], edge, lanes) for e in (entry, 1 - entry, 2))
        found.append((choose(fields, own), other, active))
    return found


def terms_kernel(plan, accumulate, cut, slots, edge, for_travellers, after, *refs):
    outputs = 2 if cut else 1
    refs, outs = refs[: len(refs) - outputs - after], refs[-outputs:]
    blocks = sum(number for number, _ in plan)
    moving, (own, home, *refs) = refs[:blocks], refs[blocks:]
    tables, before = refs[:3], refs[3:]
    held = home.shape[0] // (8 * edge)
    count = moving[0].shape[0] // (8 * edge)
    own = Fields(own.shape[0] // (8 * edge), edge, own).info()
    near = own[0:1] == (0 if for_travellers else 1)
    home = Fields(held, edge, home)
    home = [home.quadrants(j) for j in range(held)]
    found = []
    for number, arrivals in plan:
        block, moving = Fields(count, edge, *moving[:number], near=near), moving[number:]
        info = block.info() if for_travellers else own
        found += slots_of(block, info, near, arrivals, slots, 0 if for_travellers else 1)
    total = [[before[0][j, q] for q in range(4)] for j in range(held)] if accumulate else zero_total(home)
    group = 2 * slots
    for start in range(0, len(found), group):
        gather_terms(found[start : start + group], home, total, tables)
    if not cut:
        for j, field in enumerate(total):
            for q in range(4):
                outs[0][j, q] = field[q]
        return
    mine, others = outs
    rows = mine.shape[2]
    parts = edge // rows
    for k in range(parts):
        group = wide(own[1:2], rows, home[0][0].shape[1]) + k
        group = jnp.where(group >= parts, group - parts, group)
        for j, field in enumerate(total):
            cuts = [[q[p * rows : (p + 1) * rows] for q in field] for p in range(parts)]
            for q, piece in enumerate(choose(cuts, group)):
                if k == 0:
                    mine[j, q] = piece
                else:
                    others[k - 1, j, q] = piece


def unfold_table_kernel(edge, _, table):
    table[...] = fold_table(edge, True)


def gate_kernel(_, out):
    out[...] = jnp.zeros_like(out)


def sum_kernel(number, *refs):
    parts, (table, terms, trav_total, res_total) = refs[:number], refs[number:]
    fields = [[terms[j, q] for q in range(4)] for j in range(terms.shape[0])]
    for j, field in enumerate(unfold(fields, table[...])):
        res_total[j] = field
    total = []
    for j in range(parts[0].shape[0]):
        total.append([sum((part[j, q] for part in parts[1:]), parts[0][j, q]) for q in range(4)])
    for j, field in enumerate(unfold(total, table[...])):
        trav_total[j] = field


VMEM = pl.BlockSpec(memory_space=pltpu.VMEM)
HBM = pl.BlockSpec(memory_space=pl.ANY)
LIMIT = pltpu.CompilerParams(vmem_limit_bytes=32 * 1024 * 1024)
LIMIT_U = pltpu.CompilerParams(vmem_limit_bytes=60 * 1024 * 1024)
LIMIT_W = pltpu.CompilerParams(vmem_limit_bytes=32 * 1024 * 1024)


def cost(microseconds):
    return pl.CostEstimate(flops=int(microseconds * 1e9), bytes_accessed=1024, transcendentals=0)


def from_behind(value, by):
    peers = lax.axis_size("blk")
    return lax.ppermute(value, "blk", [(i, (i + by) % peers) for i in range(peers)])


def other_core(value):
    peers = lax.axis_size("blk")
    return lax.ppermute(value, "blk", [(i, i ^ 1) for i in range(peers)])


def local(residents, travellers, pair_list):
    count, edge, plane = residents.shape
    held = travellers.shape[0]
    steps, slots = pair_list.shape[1:3]
    direct = range(2, steps + 1, 2)
    arrivals = len(direct)
    groups = lax.axis_size("grp")
    part = edge // groups
    fields = 2 * slots
    small = jnp.asarray(small_tables(edge, fields))

    shapes = (
        (8 * count * edge + info_rows(steps, slots), plane // 8),
        (8 * held * edge, plane // 8),
    )
    packed, moving = pl.pallas_call(
        functools.partial(pack_kernel, ("blk", "grp")),
        out_shape=tuple(jax.ShapeDtypeStruct(shape, jnp.bfloat16) for shape in shapes),
        in_specs=[HBM, HBM, HBM],
        out_specs=(HBM, HBM),
        scratch_shapes=[
            pltpu.VMEM(residents.shape, jnp.bfloat16),
            pltpu.VMEM(travellers.shape, jnp.bfloat16),
            pltpu.SMEM((1, 3, slots, steps), jnp.int32),
            *(pltpu.VMEM(shape, jnp.bfloat16) for shape in shapes),
            pltpu.SemaphoreType.DMA((5 + count,)),
        ],
        compiler_params=LIMIT_U,
        cost_estimate=cost(1),
        name="pack",
    )(residents, travellers, jnp.transpose(pair_list, (0, 3, 2, 1)))
    tables = pl.pallas_call(
        functools.partial(tables_kernel, fields),
        out_shape=(
            jax.ShapeDtypeStruct((plane // 2, plane // 4), jnp.bfloat16),
            jax.ShapeDtypeStruct((2 * fields * edge, fields * edge), jnp.bfloat16),
            jax.ShapeDtypeStruct((edge, plane), jnp.float32),
        ),
        in_specs=[VMEM],
        out_specs=(VMEM,) * 3,
        compiler_params=LIMIT,
        cost_estimate=cost(20),
        name="tables",
    )(small)

    def stage(plan, blocks, home, total, for_travellers, microseconds, name, cut=False, after=()):
        number = home[1].shape[0] // (8 * edge)
        if cut:
            out_shape = (
                jax.ShapeDtypeStruct((number, 4, part, plane // 4), jnp.float32),
                jax.ShapeDtypeStruct((groups - 1, number, 4, part, plane // 4), jnp.float32),
            )
        else:
            out_shape = jax.ShapeDtypeStruct((number, 4, edge, plane // 4), jnp.float32)
        operands = (*blocks, *home, *tables) + (() if total is None else (total,))
        return pl.pallas_call(
            functools.partial(
                terms_kernel, plan, total is not None, cut, slots, edge, for_travellers, len(after)
            ),
            out_shape=out_shape,
            in_specs=[VMEM] * (len(operands) + len(after)),
            out_specs=jax.tree.map(lambda _: VMEM, out_shape),
            compiler_params=LIMIT,
            cost_estimate=cost(microseconds),
            name=name,
        )(*operands, *after)

    last = arrivals - 1

    def straight(k):
        return 1, (2 * k + 1, 2 * k + 1)

    middle = [(1, (2 * k + 2, 2 * k)) for k in range(last)]
    ends = [(2, (0, 2 * last))]

    res_moved = [from_behind(packed, -s) for s in direct]
    res_swapped = [other_core(packed)] + [other_core(value) for value in res_moved]
    trav_moved = [from_behind(moving, s) for s in direct]
    trav_swapped = [other_core(moving)]

    unfolding = pl.pallas_call(
        functools.partial(unfold_table_kernel, edge),
        out_shape=jax.ShapeDtypeStruct((plane // 2, plane // 2), jnp.bfloat16),
        in_specs=[HBM],
        out_specs=VMEM,
        compiler_params=LIMIT,
        cost_estimate=cost(20),
        name="unfold_table",
    )(res_moved[0])

    home = (packed, moving)
    blocks = [res_moved[last], res_swapped[0], res_swapped[-1]]
    total = stage([straight(last)] + ends, blocks, home, None, True, 10, "early_traveller_terms")
    for k in range(last):
        res_moved[k], total = lax.optimization_barrier((res_moved[k], total))
        total = stage([straight(k)], [res_moved[k]], home, total, True, 1, "middle_traveller_terms")
    blocks = [other_core(value) for value in res_moved[:last]]
    mine, others = stage(middle, blocks, home, total, True, 2, "late_traveller_terms", cut=True, after=(unfolding,))

    gate = pl.pallas_call(
        gate_kernel,
        out_shape=jax.ShapeDtypeStruct((8, 128), jnp.float32),
        in_specs=[HBM],
        out_specs=VMEM,
        compiler_params=LIMIT,
        cost_estimate=cost(1),
        name="gate",
    )(others)
    trav_moved, gate = lax.optimization_barrier((trav_moved, gate))
    trav_swapped += [other_core(value) for value in trav_moved]
    sent = [
        lax.ppermute(others[k - 1], "grp", [(g, (g + k) % groups) for g in range(groups)])
        for k in range(1, groups)
    ]
    res_total = stage(
        [straight(k) for k in range(arrivals)] + middle + ends,
        [*trav_moved, *trav_swapped[1:-1], trav_swapped[0], trav_swapped[-1]],
        (packed, packed),
        None,
        False,
        0.5,
        "resident_terms",
        after=(gate,),
    )
    res_total, sent = lax.optimization_barrier((res_total, sent))
    parts = [mine, *sent]
    trav_total, res_total = pl.pallas_call(
        functools.partial(sum_kernel, len(parts)),
        out_shape=(
            jax.ShapeDtypeStruct((held, part, plane), jnp.float32),
            jax.ShapeDtypeStruct(residents.shape, jnp.float32),
        ),
        in_specs=[VMEM] * (len(parts) + 2),
        out_specs=(VMEM, VMEM),
        compiler_params=LIMIT,
        cost_estimate=cost(0.5),
        name="sums",
    )(*parts, unfolding, res_total)
    return res_total, trav_total


def solution(mesh):
    return jax.shard_map(
        local,
        mesh=mesh,
        in_specs=(
            P(("blk", "grp"), None, None),
            P("blk", None, None),
            P(("blk", "grp"), None, None, None),
        ),
        out_specs=(P(("blk", "grp"), None, None), P("blk", "grp", None)),
        check_vma=False,
    )
```

```python
import functools

import jax
import jax.numpy as jnp
import numpy as np
from jax import lax
from jax.experimental import pallas as pl
from jax.experimental.pallas import tpu as pltpu
from jax.sharding import PartitionSpec as P


@functools.lru_cache
def small_tables(edge, fields):
    index = np.arange(edge) + 1.0
    sine = np.sqrt(2.0 / (edge + 1)) * np.sin(np.pi * np.outer(index, index) / (edge + 1))
    eigen = 2.0 - 2.0 * np.cos(np.pi * index / (edge + 1))
    part = sine[::2, ::2]
    split = (eigen[::2], eigen[::-1][::2])
    plane = [np.add.outer(split[b], split[c]).reshape(-1) for b in (0, 1) for c in (0, 1)]
    lanes = max(edge * edge // 4, 2 * fields * edge)
    rows = [
        np.repeat(part, edge // 2, axis=1),
        np.tile(part, (1, edge // 2)),
        np.concatenate([np.tile(sine, (1, fields)), np.tile(eigen[:, None], (1, fields * edge))], axis=1),
        np.stack(plane),
        np.zeros((4, 1)),
    ]
    return np.concatenate([np.pad(r, ((0, 0), (0, lanes - r.shape[1]))) for r in rows]).astype(np.float32)


def make_tables(small, edge, fields, plane_table, along, inverse):
    part, lanes, rows = edge // 2, edge * edge // 4, fields * edge
    second = small[part : 2 * part, :lanes]
    for n in range(part):
        high, low = halves(small[n : n + 1, :lanes] * second)
        plane_table[n * part : (n + 1) * part, :] = high
        plane_table[lanes + n * part : lanes + (n + 1) * part, :] = low
    sine = jnp.concatenate([small[edge : 2 * edge, :rows]] * fields, axis=0)
    row = lax.broadcasted_iota(jnp.int32, (rows, rows), 0)
    column = lax.broadcasted_iota(jnp.int32, (rows, rows), 1)
    high, low = halves(jnp.where(row // edge == column // edge, sine, 0.0))
    along[:rows, :] = high
    along[rows:, :] = low
    eigen = small[edge : 2 * edge, rows : rows + 1]
    for q in range(4):
        plane = small[2 * edge + q : 2 * edge + q + 1, :lanes]
        inverse[:, q * lanes : (q + 1) * lanes] = 1.0 / (eigen + plane)


def fold_source(lane, edge):
    small = edge // 2
    point_c = lane % small
    point_b = (lane // small) % (edge // 4)
    quadrant = lane // (small * (edge // 4))
    b = jnp.where(quadrant < 2, 2 * point_b, small - 1 - 2 * point_b)
    c = jnp.where(quadrant % 2 == 0, 2 * point_c, edge - 1 - 2 * point_c)
    return b * edge + c


def fold_table(edge, transposed):
    lanes = edge * edge // 2
    dim = 0 if transposed else 1
    folded = fold_source(lax.broadcasted_iota(jnp.int32, (lanes, 1) if transposed else (1, lanes), dim), edge)
    plain = lax.broadcasted_iota(jnp.int32, (lanes, lanes), 1 - dim)
    return jnp.where(plain == folded, 1.0, 0.0).astype(jnp.bfloat16)


def tile_of(quadrant, half):
    return 2 * quadrant + (half if quadrant < 2 else 1 - half)


def dot(x, y):
    return jnp.dot(x, y, preferred_element_type=jnp.float32)


def halves(x):
    high = x.astype(jnp.bfloat16)
    return high, (x - high.astype(jnp.float32)).astype(jnp.bfloat16)


def times_table(x, table):
    x_high, x_low = halves(x)
    high, low = table[: table.shape[0] // 2], table[table.shape[0] // 2 :]
    return dot(x_high, high) + (dot(x_low, high) + dot(x_high, low))


def table_times(table, x):
    x_high, x_low = halves(x)
    high, low = table[: table.shape[0] // 2], table[table.shape[0] // 2 :]
    return dot(
        jnp.concatenate([high, high, low], axis=1), jnp.concatenate([x_high, x_low, x_high], axis=0)
    )


def spread(quadrants):
    a, b, c, d = quadrants
    return [a + b + (c + d), a - b + (c - d), a + b - (c + d), a - b - (c - d)]


def info_rows(steps, slots):
    return -(-(steps * slots * 3 + 2) // 16) * 16


def store_folded(fields, table, target):
    count, edge, plane = fields.shape
    half, lanes = plane // 2, plane // 8
    rows = [fields[i, :, h * half : (h + 1) * half] for i in range(count) for h in (0, 1)]
    folded = dot(jnp.concatenate(rows, axis=0), table).astype(jnp.bfloat16)
    for i in range(count):
        for h in (0, 1):
            start = (2 * i + h) * edge
            for q in range(4):
                row = (tile_of(q, h) * count + i) * edge
                target[row : row + edge, :] = folded[start : start + edge, q * lanes : (q + 1) * lanes]


def pack_kernel(axes, residents, pairs, packed, fields, entries_ref, folded, sems):
    count, edge, plane = residents.shape
    loads = [pltpu.make_async_copy(residents.at[i], fields.at[i], sems.at[2 + i]) for i in range(count)]
    load_entries = pltpu.make_async_copy(pairs, entries_ref, sems.at[1])
    for load in loads:
        load.start()
    load_entries.start()
    table = fold_table(edge, False)
    load_entries.wait()
    _, entries, slots, steps = pairs.shape
    row = lax.broadcasted_iota(jnp.int32, (info_rows(steps, slots), packed.shape[1]), 0)
    values = jnp.zeros(row.shape, jnp.int32)
    scalars = [entries_ref[0, e, p, s] for s in range(steps) for p in range(slots) for e in range(entries)]
    for k, value in enumerate([lax.axis_index(axes[0]) % 2, lax.axis_index(axes[1]), *scalars]):
        values = jnp.where(row == k, value, values)
    folded[8 * count * edge :, :] = values.astype(jnp.float32).astype(jnp.bfloat16)
    for load in loads:
        load.wait()
    store_folded(fields, table, folded)
    store = pltpu.make_async_copy(folded, packed, sems.at[0])
    store.start()
    store.wait()


def tables_kernel(count, small, travellers, plane_table, along, inverse, folding, unfolding, moving):
    edge = inverse.shape[0]
    make_tables(small, edge, count, plane_table, along, inverse)
    folding[...] = fold_table(edge, False)
    unfolding[...] = fold_table(edge, True)
    store_folded(travellers, folding[...], moving)


class Fields:
    def __init__(self, count, edge, *refs, near=None):
        self.count, self.edge, self.refs, self.near = count, edge, refs, near

    def rows(self, start, size):
        values = [ref[start : start + size, :].astype(jnp.float32) for ref in self.refs]
        return jnp.where(self.near, *values) if len(values) == 2 else values[0]

    def quadrants(self, i):
        tiles = [self.rows((t * self.count + i) * self.edge, self.edge) for t in range(8)]
        return [jnp.concatenate(tiles[2 * q : 2 * q + 2], axis=1) for q in range(4)]

    def info(self, count=None):
        start = 8 * self.count * self.edge
        return self.rows(start, self.refs[0].shape[0] - start)


class PlainFields:
    def __init__(self, count, edge, *refs, near=None, table=None):
        self.count, self.edge, self.near = count, edge, near
        half = edge * edge // 2
        values = [[ref[i].astype(jnp.float32) for i in range(count)] for ref in refs]
        fields = values[0]
        if len(values) == 2:
            fields = [jnp.where(near, *pair) for pair in zip(*values)]
        rows = [field[:, h * half : (h + 1) * half] for field in fields for h in (0, 1)]
        self.folded = dot(jnp.concatenate(rows, axis=0).astype(jnp.bfloat16), table)

    def quadrants(self, i):
        edge, lanes = self.edge, self.folded.shape[1] // 4
        found = []
        for q in range(4):
            order = (0, 1) if q < 2 else (1, 0)
            tiles = [
                self.folded[(2 * i + h) * edge : (2 * i + h + 1) * edge, q * lanes : (q + 1) * lanes]
                for h in order
            ]
            found.append(jnp.concatenate(tiles, axis=1))
        return found


def wide(row, edge, lanes):
    return jnp.broadcast_to(jnp.concatenate([row] * (lanes // row.shape[1]), axis=1), (edge, lanes))


def choose(fields, index):
    chosen = fields[0]
    for i in range(1, len(fields)):
        chosen = [jnp.where(index == i, new, old) for new, old in zip(fields[i], chosen)]
    return chosen


def slot_rows(info, arrival, slots):
    start = 2 + arrival * slots * 3
    return [info[start + 3 * p : start + 3 * p + 3] for p in range(slots)]


def gather_terms(slots, home, total, tables):
    plane_table, along, inverse = (table[...] for table in tables)
    edge = inverse.shape[0]
    rows = len(slots) * edge
    densities = []
    for moving, index, _ in slots:
        densities.append(spread([m * h for m, h in zip(moving, choose(home, index))]))
    field = jnp.concatenate([density[q] for q in range(4) for density in densities], axis=0)
    field = times_table(field, plane_table)
    field = jnp.concatenate([field[q * rows : (q + 1) * rows] for q in range(4)], axis=1)
    size = along.shape[0] // 2
    along = jnp.concatenate([along[:rows, :rows], along[size : size + rows, :rows]], axis=0)
    field = table_times(along, field)
    field = (field.reshape(len(slots), edge, -1) * inverse[None]).reshape(field.shape)
    field = table_times(along, field)
    lanes = field.shape[1] // 4
    field = jnp.concatenate([field[:, q * lanes : (q + 1) * lanes] for q in range(4)], axis=0)
    field = times_table(field, plane_table)
    for slot, (moving, index, active) in enumerate(slots):
        potential = spread([field[q * rows + slot * edge : q * rows + (slot + 1) * edge] for q in range(4)])
        terms = [active * p * m for p, m in zip(potential, moving)]
        for j in range(len(home)):
            total[j] = [old + jnp.where(index == j, new, 0.0) for old, new in zip(total[j], terms)]


def zero_total(home):
    return [[jnp.zeros_like(q) for q in field] for field in home]


def unfold(fields, table):
    rows = fields[0][0].shape[0]
    lanes = table.shape[0] // 4
    stack = []
    for field in fields:
        for h in (0, 1):
            tiles = [tile_of(q, h) for q in range(4)]
            stack.append(
                jnp.concatenate(
                    [field[t // 2][:, (t % 2) * lanes : (t % 2 + 1) * lanes] for t in tiles], axis=1
                )
            )
    high, low = halves(jnp.concatenate(stack, axis=0))
    plain = dot(high, table) + dot(low, table)
    return [
        jnp.concatenate([plain[k * rows : (k + 1) * rows] for k in (2 * i, 2 * i + 1)], axis=1)
        for i in range(len(fields))
    ]


def slots_of(block, info, near, arrivals, slots, entry):
    edge = block.edge
    fields = [block.quadrants(i) for i in range(block.count)]
    lanes = fields[0][0].shape[1]
    found = []
    for row, far in zip(slot_rows(info, arrivals[0], slots), slot_rows(info, arrivals[1], slots)):
        row = jnp.where(near, row, far)
        own, other, active = (wide(row[e : e + 1], edge, lanes) for e in (entry, 1 - entry, 2))
        found.append((choose(fields, own), other, active))
    return found


def terms_kernel(plan, accumulate, cut, slots, edge, for_travellers, after, *refs):
    outputs = 2 if cut else 1
    refs, outs = refs[: len(refs) - outputs - after], refs[-outputs:]
    blocks = sum(number for number, _ in plan)
    moving, (own, home, *refs) = refs[:blocks], refs[blocks:]
    tables, folding, before = refs[:3], refs[3], refs[4:]
    held = home.shape[0] // (8 * edge)
    count = moving[0].shape[0] // (8 * edge) if for_travellers else moving[0].shape[0]
    own = Fields(own.shape[0] // (8 * edge), edge, own).info()
    near = own[0:1] == (0 if for_travellers else 1)
    home = Fields(held, edge, home)
    home = [home.quadrants(j) for j in range(held)]
    found = []
    for number, arrivals in plan:
        sources, moving = moving[:number], moving[number:]
        if for_travellers:
            block = Fields(count, edge, *sources, near=near)
        else:
            block = PlainFields(count, edge, *sources, near=near[0:1, 0:1], table=folding[...])
        info = block.info() if for_travellers else own
        found += slots_of(block, info, near, arrivals, slots, 0 if for_travellers else 1)
    total = [[before[0][j, q] for q in range(4)] for j in range(held)] if accumulate else zero_total(home)
    group = 2 * slots
    for start in range(0, len(found), group):
        gather_terms(found[start : start + group], home, total, tables)
    if not cut:
        for j, field in enumerate(total):
            for q in range(4):
                outs[0][j, q] = field[q]
        return
    mine, others = outs
    rows = mine.shape[2]
    parts = edge // rows
    for k in range(parts):
        group = wide(own[1:2], rows, home[0][0].shape[1]) + k
        group = jnp.where(group >= parts, group - parts, group)
        for j, field in enumerate(total):
            cuts = [[q[p * rows : (p + 1) * rows] for q in field] for p in range(parts)]
            for q, piece in enumerate(choose(cuts, group)):
                if k == 0:
                    mine[j, q] = piece
                else:
                    others[k - 1, j, q] = piece


def gate_kernel(_, out):
    out[...] = jnp.zeros_like(out)


def sum_kernel(number, *refs):
    parts, (table, terms, trav_total, res_total) = refs[:number], refs[number:]
    fields = [[terms[j, q] for q in range(4)] for j in range(terms.shape[0])]
    for j, field in enumerate(unfold(fields, table[...])):
        res_total[j] = field
    total = []
    for j in range(parts[0].shape[0]):
        total.append([sum((part[j, q] for part in parts[1:]), parts[0][j, q]) for q in range(4)])
    for j, field in enumerate(unfold(total, table[...])):
        trav_total[j] = field


VMEM = pl.BlockSpec(memory_space=pltpu.VMEM)
HBM = pl.BlockSpec(memory_space=pl.ANY)
LIMIT = pltpu.CompilerParams(vmem_limit_bytes=32 * 1024 * 1024)
LIMIT_U = pltpu.CompilerParams(vmem_limit_bytes=60 * 1024 * 1024)
LIMIT_W = pltpu.CompilerParams(vmem_limit_bytes=32 * 1024 * 1024)


def cost(microseconds):
    return pl.CostEstimate(flops=int(microseconds * 1e9), bytes_accessed=1024, transcendentals=0)


def from_behind(value, by):
    peers = lax.axis_size("blk")
    return lax.ppermute(value, "blk", [(i, (i + by) % peers) for i in range(peers)])


def other_core(value):
    peers = lax.axis_size("blk")
    return lax.ppermute(value, "blk", [(i, i ^ 1) for i in range(peers)])


def local(residents, travellers, pair_list):
    count, edge, plane = residents.shape
    held = travellers.shape[0]
    steps, slots = pair_list.shape[1:3]
    direct = range(2, steps + 1, 2)
    arrivals = len(direct)
    groups = lax.axis_size("grp")
    part = edge // groups
    fields = 2 * slots
    small = jnp.asarray(small_tables(edge, fields))

    shape = (8 * count * edge + info_rows(steps, slots), plane // 8)
    packed = pl.pallas_call(
        functools.partial(pack_kernel, ("blk", "grp")),
        out_shape=jax.ShapeDtypeStruct(shape, jnp.bfloat16),
        in_specs=[HBM, HBM],
        out_specs=HBM,
        scratch_shapes=[
            pltpu.VMEM(residents.shape, jnp.bfloat16),
            pltpu.SMEM((1, 3, slots, steps), jnp.int32),
            pltpu.VMEM(shape, jnp.bfloat16),
            pltpu.SemaphoreType.DMA((2 + count,)),
        ],
        compiler_params=LIMIT_U,
        cost_estimate=cost(1),
        name="pack",
    )(residents, jnp.transpose(pair_list, (0, 3, 2, 1)))
    *tables, folding, unfolding, moving = pl.pallas_call(
        functools.partial(tables_kernel, fields),
        out_shape=(
            jax.ShapeDtypeStruct((plane // 2, plane // 4), jnp.bfloat16),
            jax.ShapeDtypeStruct((2 * fields * edge, fields * edge), jnp.bfloat16),
            jax.ShapeDtypeStruct((edge, plane), jnp.float32),
            jax.ShapeDtypeStruct((plane // 2, plane // 2), jnp.bfloat16),
            jax.ShapeDtypeStruct((plane // 2, plane // 2), jnp.bfloat16),
            jax.ShapeDtypeStruct((8 * held * edge, plane // 8), jnp.bfloat16),
        ),
        in_specs=[VMEM, VMEM],
        out_specs=(VMEM,) * 6,
        compiler_params=LIMIT,
        cost_estimate=cost(20),
        name="tables",
    )(small, travellers)

    def stage(plan, blocks, home, total, for_travellers, microseconds, name, cut=False, after=()):
        number = home[1].shape[0] // (8 * edge)
        if cut:
            out_shape = (
                jax.ShapeDtypeStruct((number, 4, part, plane // 4), jnp.float32),
                jax.ShapeDtypeStruct((groups - 1, number, 4, part, plane // 4), jnp.float32),
            )
        else:
            out_shape = jax.ShapeDtypeStruct((number, 4, edge, plane // 4), jnp.float32)
        operands = (*blocks, *home, *tables, folding) + (() if total is None else (total,))
        return pl.pallas_call(
            functools.partial(
                terms_kernel, plan, total is not None, cut, slots, edge, for_travellers, len(after)
            ),
            out_shape=out_shape,
            in_specs=[VMEM] * (len(operands) + len(after)),
            out_specs=jax.tree.map(lambda _: VMEM, out_shape),
            compiler_params=LIMIT,
            cost_estimate=cost(microseconds),
            name=name,
        )(*operands, *after)

    last = arrivals - 1

    def straight(k):
        return 1, (2 * k + 1, 2 * k + 1)

    middle = [(1, (2 * k + 2, 2 * k)) for k in range(last)]
    ends = [(2, (0, 2 * last))]

    res_moved = [from_behind(packed, -s) for s in direct]
    res_swapped = [other_core(packed)] + [other_core(value) for value in res_moved]
    passed, packed_first = lax.optimization_barrier((travellers, packed))
    trav_moved = [from_behind(passed, s) for s in direct]
    trav_swapped = [other_core(passed)]

    def gate(value, microseconds):
        return pl.pallas_call(
            gate_kernel,
            out_shape=jax.ShapeDtypeStruct((8, 128), jnp.float32),
            in_specs=[HBM],
            out_specs=VMEM,
            compiler_params=LIMIT,
            cost_estimate=cost(microseconds),
            name="gate",
        )(value)

    arrived = gate(res_moved[0], 20)

    home = (packed, moving)
    blocks = [res_moved[last], res_swapped[0], res_swapped[-1]]
    total = stage([straight(last)] + ends, blocks, home, None, True, 10, "early_traveller_terms")
    for k in range(last):
        res_moved[k], total = lax.optimization_barrier((res_moved[k], total))
        total = stage([straight(k)], [res_moved[k]], home, total, True, 1, "middle_traveller_terms")
    blocks = [other_core(value) for value in res_moved[:last]]
    mine, others = stage(middle, blocks, home, total, True, 2, "late_traveller_terms", cut=True, after=(arrived,))

    summed = gate(others, 1)
    trav_moved, summed = lax.optimization_barrier((trav_moved, summed))
    trav_swapped += [other_core(value) for value in trav_moved]
    sent = [
        lax.ppermute(others[k - 1], "grp", [(g, (g + k) % groups) for g in range(groups)])
        for k in range(1, groups)
    ]
    res_total = stage(
        [straight(k) for k in range(arrivals)] + middle + ends,
        [*trav_moved, *trav_swapped[1:-1], trav_swapped[0], trav_swapped[-1]],
        (packed, packed),
        None,
        False,
        0.5,
        "resident_terms",
        after=(summed,),
    )
    res_total, sent = lax.optimization_barrier((res_total, sent))
    parts = [mine, *sent]
    trav_total, res_total = pl.pallas_call(
        functools.partial(sum_kernel, len(parts)),
        out_shape=(
            jax.ShapeDtypeStruct((held, part, plane), jnp.float32),
            jax.ShapeDtypeStruct(residents.shape, jnp.float32),
        ),
        in_specs=[VMEM] * (len(parts) + 2),
        out_specs=(VMEM, VMEM),
        compiler_params=LIMIT,
        cost_estimate=cost(0.5),
        name="sums",
    )(*parts, unfolding, res_total)
    return res_total, trav_total


def solution(mesh):
    return jax.shard_map(
        local,
        mesh=mesh,
        in_specs=(
            P(("blk", "grp"), None, None),
            P("blk", None, None),
            P(("blk", "grp"), None, None, None),
        ),
        out_specs=(P(("blk", "grp"), None, None), P("blk", "grp", None)),
        check_vma=False,
    )
```

```python
import functools

import jax
import jax.numpy as jnp
import numpy as np
from jax import lax
from jax.experimental import pallas as pl
from jax.experimental.pallas import tpu as pltpu
from jax.sharding import PartitionSpec as P


SPARE_ROWS = 8


@functools.lru_cache
def small_tables(edge, fields):
    index = np.arange(edge) + 1.0
    sine = np.sqrt(2.0 / (edge + 1)) * np.sin(np.pi * np.outer(index, index) / (edge + 1))
    eigen = 2.0 - 2.0 * np.cos(np.pi * index / (edge + 1))
    part = sine[::2, ::2]
    split = (eigen[::2], eigen[::-1][::2])
    plane = [np.add.outer(split[b], split[c]).reshape(-1) for b in (0, 1) for c in (0, 1)]
    lanes = max(edge * edge // 4, 2 * fields * edge)
    rows = [
        np.repeat(part, edge // 2, axis=1),
        np.tile(part, (1, edge // 2)),
        np.concatenate([np.tile(sine, (1, fields)), np.tile(eigen[:, None], (1, fields * edge))], axis=1),
        np.stack(plane),
        np.zeros((4, 1)),
    ]
    return np.concatenate([np.pad(r, ((0, 0), (0, lanes - r.shape[1]))) for r in rows]).astype(np.float32)


def make_tables(small, edge, fields, plane_table, along, inverse):
    part, lanes, rows = edge // 2, edge * edge // 4, fields * edge
    second = small[part : 2 * part, :lanes]
    for n in range(part):
        high, low = halves(small[n : n + 1, :lanes] * second)
        plane_table[n * part : (n + 1) * part, :] = high
        plane_table[lanes + n * part : lanes + (n + 1) * part, :] = low
    sine = jnp.concatenate([small[edge : 2 * edge, :rows]] * fields, axis=0)
    row = lax.broadcasted_iota(jnp.int32, (rows, rows), 0)
    column = lax.broadcasted_iota(jnp.int32, (rows, rows), 1)
    high, low = halves(jnp.where(row // edge == column // edge, sine, 0.0))
    along[:rows, :] = high
    along[rows:, :] = low
    eigen = small[edge : 2 * edge, rows : rows + 1]
    for q in range(4):
        plane = small[2 * edge + q : 2 * edge + q + 1, :lanes]
        inverse[:, q * lanes : (q + 1) * lanes] = 1.0 / (eigen + plane)


def fold_source(lane, edge):
    small = edge // 2
    point_c = lane % small
    point_b = (lane // small) % (edge // 4)
    quadrant = lane // (small * (edge // 4))
    b = jnp.where(quadrant < 2, 2 * point_b, small - 1 - 2 * point_b)
    c = jnp.where(quadrant % 2 == 0, 2 * point_c, edge - 1 - 2 * point_c)
    return b * edge + c


def fold_table(edge, transposed):
    lanes = edge * edge // 2
    dim = 0 if transposed else 1
    folded = fold_source(lax.broadcasted_iota(jnp.int32, (lanes, 1) if transposed else (1, lanes), dim), edge)
    plain = lax.broadcasted_iota(jnp.int32, (lanes, lanes), 1 - dim)
    return jnp.where(plain == folded, 1.0, 0.0).astype(jnp.bfloat16)


def tile_of(quadrant, half):
    return 2 * quadrant + (half if quadrant < 2 else 1 - half)


def dot(x, y):
    return jnp.dot(x, y, preferred_element_type=jnp.float32)


def halves(x):
    high = x.astype(jnp.bfloat16)
    return high, (x - high.astype(jnp.float32)).astype(jnp.bfloat16)


def times_table(x, table):
    x_high, x_low = halves(x)
    high, low = table[: table.shape[0] // 2], table[table.shape[0] // 2 :]
    return dot(x_high, high) + (dot(x_low, high) + dot(x_high, low))


def table_times(table, x):
    x_high, x_low = halves(x)
    high, low = table[: table.shape[0] // 2], table[table.shape[0] // 2 :]
    return dot(
        jnp.concatenate([high, high, low], axis=1), jnp.concatenate([x_high, x_low, x_high], axis=0)
    )


def spread(quadrants):
    a, b, c, d = quadrants
    return [a + b + (c + d), a - b + (c - d), a + b - (c + d), a - b - (c - d)]


def info_rows(steps, slots):
    return -(-(steps * slots * 3 + 2) // 16) * 16


def store_folded(fields, table, target):
    count, edge, plane = fields.shape
    half, lanes = plane // 2, plane // 8
    rows = [fields[i, :, h * half : (h + 1) * half] for i in range(count) for h in (0, 1)]
    folded = dot(jnp.concatenate(rows, axis=0), table).astype(jnp.bfloat16)
    for i in range(count):
        for h in (0, 1):
            start = (2 * i + h) * edge
            for q in range(4):
                row = (tile_of(q, h) * count + i) * edge
                target[row : row + edge, :] = folded[start : start + edge, q * lanes : (q + 1) * lanes]


def pack_kernel(axes, residents, pairs, packed, fields, entries_ref, folded, sems):
    count, edge, plane = residents.shape
    loads = [pltpu.make_async_copy(residents.at[i], fields.at[i], sems.at[2 + i]) for i in range(count)]
    load_entries = pltpu.make_async_copy(pairs, entries_ref, sems.at[1])
    for load in loads:
        load.start()
    load_entries.start()
    table = fold_table(edge, False)
    load_entries.wait()
    _, entries, slots, steps = pairs.shape
    row = lax.broadcasted_iota(jnp.int32, (info_rows(steps, slots), packed.shape[1]), 0)
    values = jnp.zeros(row.shape, jnp.int32)
    scalars = [entries_ref[0, e, p, s] for s in range(steps) for p in range(slots) for e in range(entries)]
    for k, value in enumerate([lax.axis_index(axes[0]) % 2, lax.axis_index(axes[1]), *scalars]):
        values = jnp.where(row == k, value, values)
    folded[8 * count * edge :, :] = values.astype(jnp.float32).astype(jnp.bfloat16)
    for load in loads:
        load.wait()
    store_folded(fields, table, folded)
    store = pltpu.make_async_copy(folded, packed, sems.at[0])
    store.start()
    store.wait()


def tables_kernel(count, small, travellers, plane_table, along, inverse, folding, unfolding, moving):
    edge = inverse.shape[0]
    make_tables(small, edge, count, plane_table, along, inverse)
    folding[...] = fold_table(edge, False)
    unfolding[...] = fold_table(edge, True)
    store_folded(travellers, folding[...], moving)


class Fields:
    def __init__(self, count, edge, *refs, near=None):
        self.count, self.edge, self.refs, self.near = count, edge, refs, near

    def rows(self, start, size):
        values = [ref[start : start + size, :].astype(jnp.float32) for ref in self.refs]
        return jnp.where(self.near, *values) if len(values) == 2 else values[0]

    def quadrants(self, i):
        tiles = [self.rows((t * self.count + i) * self.edge, self.edge) for t in range(8)]
        return [jnp.concatenate(tiles[2 * q : 2 * q + 2], axis=1) for q in range(4)]

    def info(self, count=None):
        start = 8 * self.count * self.edge
        return self.rows(start, self.refs[0].shape[0] - start)


class PlainFields:
    def __init__(self, count, edge, *refs, near=None, table=None):
        self.count, self.edge, self.near = count, edge, near
        half = edge * edge // 2
        values = [[ref[i].astype(jnp.float32) for i in range(count)] for ref in refs]
        fields = values[0]
        if len(values) == 2:
            fields = [jnp.where(near, *pair) for pair in zip(*values)]
        rows = [field[:, h * half : (h + 1) * half] for field in fields for h in (0, 1)]
        self.folded = dot(jnp.concatenate(rows, axis=0).astype(jnp.bfloat16), table)

    def quadrants(self, i):
        edge, lanes = self.edge, self.folded.shape[1] // 4
        found = []
        for q in range(4):
            order = (0, 1) if q < 2 else (1, 0)
            tiles = [
                self.folded[(2 * i + h) * edge : (2 * i + h + 1) * edge, q * lanes : (q + 1) * lanes]
                for h in order
            ]
            found.append(jnp.concatenate(tiles, axis=1))
        return found


def wide(row, edge, lanes):
    return jnp.broadcast_to(jnp.concatenate([row] * (lanes // row.shape[1]), axis=1), (edge, lanes))


def choose(fields, index):
    chosen = fields[0]
    for i in range(1, len(fields)):
        chosen = [jnp.where(index == i, new, old) for new, old in zip(fields[i], chosen)]
    return chosen


def slot_rows(info, arrival, slots):
    start = 2 + arrival * slots * 3
    return [info[start + 3 * p : start + 3 * p + 3] for p in range(slots)]


def gather_terms(slots, home, total, tables):
    plane_table, along, inverse = (table[...] for table in tables)
    edge = inverse.shape[0]
    rows = len(slots) * edge
    densities = []
    for moving, index, _ in slots:
        densities.append(spread([m * h for m, h in zip(moving, choose(home, index))]))
    field = jnp.concatenate([density[q] for q in range(4) for density in densities], axis=0)
    field = times_table(field, plane_table)
    field = jnp.concatenate([field[q * rows : (q + 1) * rows] for q in range(4)], axis=1)
    size = along.shape[0] // 2
    along = jnp.concatenate([along[:rows, :rows], along[size : size + rows, :rows]], axis=0)
    field = table_times(along, field)
    field = (field.reshape(len(slots), edge, -1) * inverse[None]).reshape(field.shape)
    field = table_times(along, field)
    lanes = field.shape[1] // 4
    field = jnp.concatenate([field[:, q * lanes : (q + 1) * lanes] for q in range(4)], axis=0)
    field = times_table(field, plane_table)
    for slot, (moving, index, active) in enumerate(slots):
        potential = spread([field[q * rows + slot * edge : q * rows + (slot + 1) * edge] for q in range(4)])
        terms = [active * p * m for p, m in zip(potential, moving)]
        for j in range(len(home)):
            total[j] = [old + jnp.where(index == j, new, 0.0) for old, new in zip(total[j], terms)]


def zero_total(home):
    return [[jnp.zeros_like(q) for q in field] for field in home]


def unfold(fields, table):
    rows = fields[0][0].shape[0]
    lanes = table.shape[0] // 4
    stack = []
    for field in fields:
        for h in (0, 1):
            tiles = [tile_of(q, h) for q in range(4)]
            stack.append(
                jnp.concatenate(
                    [field[t // 2][:, (t % 2) * lanes : (t % 2 + 1) * lanes] for t in tiles], axis=1
                )
            )
    high, low = halves(jnp.concatenate(stack, axis=0))
    plain = dot(high, table) + dot(low, table)
    return [
        jnp.concatenate([plain[k * rows : (k + 1) * rows] for k in (2 * i, 2 * i + 1)], axis=1)
        for i in range(len(fields))
    ]


def slots_of(block, info, near, arrivals, slots, entry):
    edge = block.edge
    fields = [block.quadrants(i) for i in range(block.count)]
    lanes = fields[0][0].shape[1]
    found = []
    for row, far in zip(slot_rows(info, arrivals[0], slots), slot_rows(info, arrivals[1], slots)):
        row = jnp.where(near, row, far)
        own, other, active = (wide(row[e : e + 1], edge, lanes) for e in (entry, 1 - entry, 2))
        found.append((choose(fields, own), other, active))
    return found


def terms_kernel(plan, accumulate, cut, slots, edge, for_travellers, after, *refs):
    outputs = 2 if cut else 1
    refs, outs = refs[: len(refs) - outputs - after], refs[-outputs:]
    blocks = sum(number for number, _ in plan)
    moving, (own, home, *refs) = refs[:blocks], refs[blocks:]
    tables, folding, before = refs[:3], refs[3], refs[4:]
    held = home.shape[0] // (8 * edge)
    count = moving[0].shape[0] // (8 * edge) if for_travellers else moving[0].shape[0]
    own = Fields(own.shape[0] // (8 * edge), edge, own).info()
    near = own[0:1] == (0 if for_travellers else 1)
    home = Fields(held, edge, home)
    home = [home.quadrants(j) for j in range(held)]
    found = []
    for number, arrivals in plan:
        sources, moving = moving[:number], moving[number:]
        if for_travellers:
            block = Fields(count, edge, *sources, near=near)
        else:
            block = PlainFields(count, edge, *sources, near=near[0:1, 0:1], table=folding[...])
        info = block.info() if for_travellers else own
        found += slots_of(block, info, near, arrivals, slots, 0 if for_travellers else 1)
    total = [[before[0][j, q] for q in range(4)] for j in range(held)] if accumulate else zero_total(home)
    group = 2 * slots
    for start in range(0, len(found), group):
        gather_terms(found[start : start + group], home, total, tables)
    if not cut:
        for j, field in enumerate(total):
            for q in range(4):
                outs[0][j, q] = field[q]
        return
    mine, others = outs
    others[...] = jnp.zeros_like(others)
    rows = mine.shape[2]
    parts = edge // rows
    for k in range(parts):
        group = wide(own[1:2], rows, home[0][0].shape[1]) + k
        group = jnp.where(group >= parts, group - parts, group)
        for j, field in enumerate(total):
            cuts = [[q[p * rows : (p + 1) * rows] for q in field] for p in range(parts)]
            for q, piece in enumerate(choose(cuts, group)):
                if k == 0:
                    mine[j, q] = piece
                else:
                    others[k - 1, (4 * j + q) * rows : (4 * j + q + 1) * rows, :] = piece


def gate_kernel(_, out):
    out[...] = jnp.zeros_like(out)


def sum_kernel(number, *refs):
    parts, (table, terms, trav_total, res_total) = refs[:number], refs[number:]
    fields = [[terms[j, q] for q in range(4)] for j in range(terms.shape[0])]
    for j, field in enumerate(unfold(fields, table[...])):
        res_total[j] = field
    total = []
    size = parts[0].shape[2]
    for j in range(parts[0].shape[0]):
        starts = [(4 * j + q) * size for q in range(4)]
        total.append([sum((part[k : k + size, :] for part in parts[1:]), parts[0][j, q]) for q, k in enumerate(starts)])
    for j, field in enumerate(unfold(total, table[...])):
        trav_total[j] = field


VMEM = pl.BlockSpec(memory_space=pltpu.VMEM)
HBM = pl.BlockSpec(memory_space=pl.ANY)
LIMIT = pltpu.CompilerParams(vmem_limit_bytes=32 * 1024 * 1024)
LIMIT_U = pltpu.CompilerParams(vmem_limit_bytes=60 * 1024 * 1024)
LIMIT_W = pltpu.CompilerParams(vmem_limit_bytes=32 * 1024 * 1024)


def cost(microseconds):
    return pl.CostEstimate(flops=int(microseconds * 1e9), bytes_accessed=1024, transcendentals=0)


def from_behind(value, by):
    peers = lax.axis_size("blk")
    return lax.ppermute(value, "blk", [(i, (i + by) % peers) for i in range(peers)])


def other_core(value):
    peers = lax.axis_size("blk")
    return lax.ppermute(value, "blk", [(i, i ^ 1) for i in range(peers)])


def local(residents, travellers, pair_list):
    count, edge, plane = residents.shape
    held = travellers.shape[0]
    steps, slots = pair_list.shape[1:3]
    direct = range(2, steps + 1, 2)
    arrivals = len(direct)
    groups = lax.axis_size("grp")
    part = edge // groups
    fields = 2 * slots
    small = jnp.asarray(small_tables(edge, fields))

    shape = (8 * count * edge + info_rows(steps, slots), plane // 8)
    packed = pl.pallas_call(
        functools.partial(pack_kernel, ("blk", "grp")),
        out_shape=jax.ShapeDtypeStruct(shape, jnp.bfloat16),
        in_specs=[HBM, HBM],
        out_specs=HBM,
        scratch_shapes=[
            pltpu.VMEM(residents.shape, jnp.bfloat16),
            pltpu.SMEM((1, 3, slots, steps), jnp.int32),
            pltpu.VMEM(shape, jnp.bfloat16),
            pltpu.SemaphoreType.DMA((2 + count,)),
        ],
        compiler_params=LIMIT_U,
        cost_estimate=cost(1),
        name="pack",
    )(residents, jnp.transpose(pair_list, (0, 3, 2, 1)))
    *tables, folding, unfolding, moving = pl.pallas_call(
        functools.partial(tables_kernel, fields),
        out_shape=(
            jax.ShapeDtypeStruct((plane // 2, plane // 4), jnp.bfloat16),
            jax.ShapeDtypeStruct((2 * fields * edge, fields * edge), jnp.bfloat16),
            jax.ShapeDtypeStruct((edge, plane), jnp.float32),
            jax.ShapeDtypeStruct((plane // 2, plane // 2), jnp.bfloat16),
            jax.ShapeDtypeStruct((plane // 2, plane // 2), jnp.bfloat16),
            jax.ShapeDtypeStruct((8 * held * edge, plane // 8), jnp.bfloat16),
        ),
        in_specs=[VMEM, VMEM],
        out_specs=(VMEM,) * 6,
        compiler_params=LIMIT,
        cost_estimate=cost(20),
        name="tables",
    )(small, travellers)

    def stage(plan, blocks, home, total, for_travellers, microseconds, name, cut=False, after=()):
        number = home[1].shape[0] // (8 * edge)
        if cut:
            out_shape = (
                jax.ShapeDtypeStruct((number, 4, part, plane // 4), jnp.float32),
                jax.ShapeDtypeStruct((groups - 1, number * 4 * part + SPARE_ROWS, plane // 4), jnp.float32),
            )
        else:
            out_shape = jax.ShapeDtypeStruct((number, 4, edge, plane // 4), jnp.float32)
        operands = (*blocks, *home, *tables, folding) + (() if total is None else (total,))
        return pl.pallas_call(
            functools.partial(
                terms_kernel, plan, total is not None, cut, slots, edge, for_travellers, len(after)
            ),
            out_shape=out_shape,
            in_specs=[VMEM] * (len(operands) + len(after)),
            out_specs=jax.tree.map(lambda _: VMEM, out_shape),
            compiler_params=LIMIT,
            cost_estimate=cost(microseconds),
            name=name,
        )(*operands, *after)

    last = arrivals - 1

    def straight(k):
        return 1, (2 * k + 1, 2 * k + 1)

    middle = [(1, (2 * k + 2, 2 * k)) for k in range(last)]
    ends = [(2, (0, 2 * last))]

    res_moved = [from_behind(packed, -s) for s in direct]
    res_moved[last], own, moving = lax.optimization_barrier((res_moved[last], packed, moving))
    res_swapped = [other_core(own)] + [other_core(value) for value in res_moved]
    passed, packed_first = lax.optimization_barrier((travellers, packed))
    trav_moved = [from_behind(passed, s) for s in direct]
    trav_swapped = [other_core(passed)]

    def gate(value, microseconds):
        return pl.pallas_call(
            gate_kernel,
            out_shape=jax.ShapeDtypeStruct((8, 128), jnp.float32),
            in_specs=[HBM],
            out_specs=VMEM,
            compiler_params=LIMIT,
            cost_estimate=cost(microseconds),
            name="gate",
        )(value)

    arrived = gate(res_moved[0], 20)

    home = (packed, moving)
    total = stage([straight(last)], [res_moved[last]], home, None, True, 10, "first_traveller_terms")
    blocks = [res_swapped[0], res_swapped[-1]]
    total = stage(ends, blocks, home, total, True, 10, "early_traveller_terms")
    for k in range(last):
        res_moved[k], total = lax.optimization_barrier((res_moved[k], total))
        total = stage([straight(k)], [res_moved[k]], home, total, True, 1, "middle_traveller_terms")
    blocks = [other_core(value) for value in res_moved[:last]]
    mine, others = stage(middle, blocks, home, total, True, 2, "late_traveller_terms", cut=True, after=(arrived,))

    summed = gate(others, 1)
    trav_moved, summed = lax.optimization_barrier((trav_moved, summed))
    trav_swapped += [other_core(value) for value in trav_moved]
    sent = [
        lax.ppermute(others[k - 1], "grp", [(g, (g + k) % groups) for g in range(groups)])
        for k in range(1, groups)
    ]
    home = (packed, packed)
    total = stage(
        [straight(k) for k in range(arrivals)],
        trav_moved,
        home,
        None,
        False,
        0.001,
        "early_resident_terms",
        after=(summed,),
    )
    blocks = [*trav_swapped[1:-1], trav_swapped[0], trav_swapped[-1]]
    res_total = stage(middle + ends, blocks, home, total, False, 0.001, "late_resident_terms")
    res_total, sent = lax.optimization_barrier((res_total, sent))
    parts = [mine, *sent]
    trav_total, res_total = pl.pallas_call(
        functools.partial(sum_kernel, len(parts)),
        out_shape=(
            jax.ShapeDtypeStruct((held, part, plane), jnp.float32),
            jax.ShapeDtypeStruct(residents.shape, jnp.float32),
        ),
        in_specs=[VMEM] * (len(parts) + 2),
        out_specs=(VMEM, VMEM),
        compiler_params=LIMIT,
        cost_estimate=cost(0.5),
        name="sums",
    )(*parts, unfolding, res_total)
    return res_total, trav_total


def solution(mesh):
    return jax.shard_map(
        local,
        mesh=mesh,
        in_specs=(
            P(("blk", "grp"), None, None),
            P("blk", None, None),
            P(("blk", "grp"), None, None, None),
        ),
        out_specs=(P(("blk", "grp"), None, None), P("blk", "grp", None)),
        check_vma=False,
    )
```

```python
import functools

import jax
import jax.numpy as jnp
import numpy as np
from jax import lax
from jax.experimental import pallas as pl
from jax.experimental.pallas import tpu as pltpu
from jax.sharding import PartitionSpec as P


SPARE_ROWS = 8
LANES = 128


@functools.lru_cache
def small_tables(edge, fields):
    index = np.arange(edge) + 1.0
    sine = np.sqrt(2.0 / (edge + 1)) * np.sin(np.pi * np.outer(index, index) / (edge + 1))
    eigen = 2.0 - 2.0 * np.cos(np.pi * index / (edge + 1))
    part = sine[::2, ::2]
    split = (eigen[::2], eigen[::-1][::2])
    plane = [np.add.outer(split[b], split[c]).reshape(-1) for b in (0, 1) for c in (0, 1)]
    lanes = max(edge * edge // 4, 2 * fields * edge)
    rows = [
        np.repeat(part, edge // 2, axis=1),
        np.tile(part, (1, edge // 2)),
        np.concatenate([np.tile(sine, (1, fields)), np.tile(eigen[:, None], (1, fields * edge))], axis=1),
        np.stack(plane),
        np.zeros((4, 1)),
    ]
    return np.concatenate([np.pad(r, ((0, 0), (0, lanes - r.shape[1]))) for r in rows]).astype(np.float32)


def make_tables(small, edge, fields, plane_table, along, inverse):
    part, lanes, rows = edge // 2, edge * edge // 4, fields * edge
    second = small[part : 2 * part, :lanes]
    for n in range(part):
        high, low = halves(small[n : n + 1, :lanes] * second)
        plane_table[n * part : (n + 1) * part, :] = high
        plane_table[lanes + n * part : lanes + (n + 1) * part, :] = low
    sine = jnp.concatenate([small[edge : 2 * edge, :rows]] * fields, axis=0)
    row = lax.broadcasted_iota(jnp.int32, (rows, rows), 0)
    column = lax.broadcasted_iota(jnp.int32, (rows, rows), 1)
    high, low = halves(jnp.where(row // edge == column // edge, sine, 0.0))
    along[:rows, :] = high
    along[rows:, :] = low
    eigen = small[edge : 2 * edge, rows : rows + 1]
    for q in range(4):
        plane = small[2 * edge + q : 2 * edge + q + 1, :lanes]
        inverse[:, q * lanes : (q + 1) * lanes] = 1.0 / (eigen + plane)


def fold_source(lane, edge):
    small = edge // 2
    point_c = lane % small
    point_b = (lane // small) % (edge // 4)
    quadrant = lane // (small * (edge // 4))
    b = jnp.where(quadrant < 2, 2 * point_b, small - 1 - 2 * point_b)
    c = jnp.where(quadrant % 2 == 0, 2 * point_c, edge - 1 - 2 * point_c)
    return b * edge + c


def fold_table(edge, transposed):
    lanes = edge * edge // 2
    dim = 0 if transposed else 1
    folded = fold_source(lax.broadcasted_iota(jnp.int32, (lanes, 1) if transposed else (1, lanes), dim), edge)
    plain = lax.broadcasted_iota(jnp.int32, (lanes, lanes), 1 - dim)
    return jnp.where(plain == folded, 1.0, 0.0).astype(jnp.bfloat16)


def tile_of(quadrant, half):
    return 2 * quadrant + (half if quadrant < 2 else 1 - half)


def dot(x, y):
    return jnp.dot(x, y, preferred_element_type=jnp.float32)


def halves(x):
    high = x.astype(jnp.bfloat16)
    return high, (x - high.astype(jnp.float32)).astype(jnp.bfloat16)


def times_table(x, table):
    high, low = table[: table.shape[0] // 2], table[table.shape[0] // 2 :]
    parts = []
    for start in range(0, x.shape[0], LANES):
        x_high, x_low = halves(x[start : start + LANES])
        parts.append(dot(x_high, high) + (dot(x_low, high) + dot(x_high, low)))
    return jnp.concatenate(parts, axis=0)


def table_times(table, x):
    high, low = table[: table.shape[0] // 2], table[table.shape[0] // 2 :]
    table = jnp.concatenate([high, high, low], axis=1)
    parts = []
    for start in range(0, x.shape[1], 2 * LANES):
        x_high, x_low = halves(x[:, start : start + 2 * LANES])
        parts.append(dot(table, jnp.concatenate([x_high, x_low, x_high], axis=0)))
    return jnp.concatenate(parts, axis=1)


def spread(quadrants):
    a, b, c, d = quadrants
    return [a + b + (c + d), a - b + (c - d), a + b - (c + d), a - b - (c - d)]


def info_rows(steps, slots):
    return -(-(steps * slots * 3 + 2) // 16) * 16


def store_folded(fields, table, target):
    count, edge, plane = fields.shape
    half, lanes = plane // 2, plane // 8
    rows = [fields[i, :, h * half : (h + 1) * half] for i in range(count) for h in (0, 1)]
    folded = dot(jnp.concatenate(rows, axis=0), table).astype(jnp.bfloat16)
    for i in range(count):
        for h in (0, 1):
            start = (2 * i + h) * edge
            for q in range(4):
                row = (tile_of(q, h) * count + i) * edge
                target[row : row + edge, :] = folded[start : start + edge, q * lanes : (q + 1) * lanes]


def pack_kernel(axes, residents, pairs, packed, fields, entries_ref, folded, sems):
    count, edge, plane = residents.shape
    loads = [pltpu.make_async_copy(residents.at[i], fields.at[i], sems.at[2 + i]) for i in range(count)]
    load_entries = pltpu.make_async_copy(pairs, entries_ref, sems.at[1])
    for load in loads:
        load.start()
    load_entries.start()
    table = fold_table(edge, False)
    load_entries.wait()
    _, entries, slots, steps = pairs.shape
    row = lax.broadcasted_iota(jnp.int32, (info_rows(steps, slots), packed.shape[1]), 0)
    values = jnp.zeros(row.shape, jnp.int32)
    scalars = [entries_ref[0, e, p, s] for s in range(steps) for p in range(slots) for e in range(entries)]
    for k, value in enumerate([lax.axis_index(axes[0]) % 2, lax.axis_index(axes[1]), *scalars]):
        values = jnp.where(row == k, value, values)
    folded[8 * count * edge :, :] = values.astype(jnp.float32).astype(jnp.bfloat16)
    for load in loads:
        load.wait()
    store_folded(fields, table, folded)
    store = pltpu.make_async_copy(folded, packed, sems.at[0])
    store.start()
    store.wait()


def tables_kernel(count, small, travellers, plane_table, along, inverse, folding, unfolding, moving):
    edge = inverse.shape[0]
    make_tables(small, edge, count, plane_table, along, inverse)
    folding[...] = fold_table(edge, False)
    unfolding[...] = fold_table(edge, True)
    store_folded(travellers, folding[...], moving)


class Fields:
    def __init__(self, count, edge, *refs, near=None):
        self.count, self.edge, self.refs, self.near = count, edge, refs, near

    def rows(self, start, size):
        values = [ref[start : start + size, :].astype(jnp.float32) for ref in self.refs]
        return jnp.where(self.near, *values) if len(values) == 2 else values[0]

    def quadrants(self, i):
        tiles = [self.rows((t * self.count + i) * self.edge, self.edge) for t in range(8)]
        return [jnp.concatenate(tiles[2 * q : 2 * q + 2], axis=1) for q in range(4)]

    def info(self, count=None):
        start = 8 * self.count * self.edge
        return self.rows(start, self.refs[0].shape[0] - start)


class PlainFields:
    def __init__(self, count, edge, *refs, near=None, table=None):
        self.count, self.edge, self.near = count, edge, near
        half = edge * edge // 2
        values = [[ref[i].astype(jnp.float32) for i in range(count)] for ref in refs]
        fields = values[0]
        if len(values) == 2:
            fields = [jnp.where(near, *pair) for pair in zip(*values)]
        rows = [field[:, h * half : (h + 1) * half] for field in fields for h in (0, 1)]
        self.folded = dot(jnp.concatenate(rows, axis=0).astype(jnp.bfloat16), table)

    def quadrants(self, i):
        edge, lanes = self.edge, self.folded.shape[1] // 4
        found = []
        for q in range(4):
            order = (0, 1) if q < 2 else (1, 0)
            tiles = [
                self.folded[(2 * i + h) * edge : (2 * i + h + 1) * edge, q * lanes : (q + 1) * lanes]
                for h in order
            ]
            found.append(jnp.concatenate(tiles, axis=1))
        return found


def wide(row, edge, lanes):
    return jnp.broadcast_to(jnp.concatenate([row] * (lanes // row.shape[1]), axis=1), (edge, lanes))


def choose(fields, index):
    chosen = fields[0]
    for i in range(1, len(fields)):
        chosen = [jnp.where(index == i, new, old) for new, old in zip(fields[i], chosen)]
    return chosen


def slot_rows(info, arrival, slots):
    start = 2 + arrival * slots * 3
    return [info[start + 3 * p : start + 3 * p + 3] for p in range(slots)]


def gather_terms(slots, home, total, tables):
    plane_table, along, inverse = (table[...] for table in tables)
    edge = inverse.shape[0]
    rows = len(slots) * edge
    densities = []
    for moving, index, _ in slots:
        densities.append(spread([m * h for m, h in zip(moving, choose(home, index))]))
    field = jnp.concatenate([density[q] for q in range(4) for density in densities], axis=0)
    field = times_table(field, plane_table)
    field = jnp.concatenate([field[q * rows : (q + 1) * rows] for q in range(4)], axis=1)
    size = along.shape[0] // 2
    along = jnp.concatenate([along[:rows, :rows], along[size : size + rows, :rows]], axis=0)
    field = table_times(along, field)
    field = (field.reshape(len(slots), edge, -1) * inverse[None]).reshape(field.shape)
    field = table_times(along, field)
    lanes = field.shape[1] // 4
    field = jnp.concatenate([field[:, q * lanes : (q + 1) * lanes] for q in range(4)], axis=0)
    field = times_table(field, plane_table)
    for slot, (moving, index, active) in enumerate(slots):
        potential = spread([field[q * rows + slot * edge : q * rows + (slot + 1) * edge] for q in range(4)])
        terms = [active * p * m for p, m in zip(potential, moving)]
        for j in range(len(home)):
            total[j] = [old + jnp.where(index == j, new, 0.0) for old, new in zip(total[j], terms)]


def zero_total(home):
    return [[jnp.zeros_like(q) for q in field] for field in home]


def unfold(fields, table):
    rows = fields[0][0].shape[0]
    lanes = table.shape[0] // 4
    stack = []
    for field in fields:
        for h in (0, 1):
            tiles = [tile_of(q, h) for q in range(4)]
            stack.append(
                jnp.concatenate(
                    [field[t // 2][:, (t % 2) * lanes : (t % 2 + 1) * lanes] for t in tiles], axis=1
                )
            )
    high, low = halves(jnp.concatenate(stack, axis=0))
    plain = dot(high, table) + dot(low, table)
    return [
        jnp.concatenate([plain[k * rows : (k + 1) * rows] for k in (2 * i, 2 * i + 1)], axis=1)
        for i in range(len(fields))
    ]


def slots_of(block, info, near, arrivals, slots, entry):
    edge = block.edge
    fields = [block.quadrants(i) for i in range(block.count)]
    lanes = fields[0][0].shape[1]
    found = []
    for row, far in zip(slot_rows(info, arrivals[0], slots), slot_rows(info, arrivals[1], slots)):
        row = jnp.where(near, row, far)
        own, other, active = (wide(row[e : e + 1], edge, lanes) for e in (entry, 1 - entry, 2))
        found.append((choose(fields, own), other, active))
    return found


def terms_kernel(plan, accumulate, cut, slots, edge, for_travellers, after, *refs):
    outputs = 2 if cut else 1
    refs, outs = refs[: len(refs) - outputs - after], refs[-outputs:]
    blocks = sum(number for number, _ in plan)
    moving, (own, home, *refs) = refs[:blocks], refs[blocks:]
    tables, folding, before = refs[:3], refs[3], refs[4:]
    held = home.shape[0] // (8 * edge)
    count = moving[0].shape[0] // (8 * edge) if for_travellers else moving[0].shape[0]
    own = Fields(own.shape[0] // (8 * edge), edge, own).info()
    near = own[0:1] == (0 if for_travellers else 1)
    home = Fields(held, edge, home)
    home = [home.quadrants(j) for j in range(held)]
    found = []
    for number, arrivals in plan:
        sources, moving = moving[:number], moving[number:]
        if for_travellers:
            block = Fields(count, edge, *sources, near=near)
        else:
            block = PlainFields(count, edge, *sources, near=near[0:1, 0:1], table=folding[...])
        info = block.info() if for_travellers else own
        found += slots_of(block, info, near, arrivals, slots, 0 if for_travellers else 1)
    total = [[before[0][j, q] for q in range(4)] for j in range(held)] if accumulate else zero_total(home)
    group = 2 * slots
    for start in range(0, len(found), group):
        gather_terms(found[start : start + group], home, total, tables)
    if not cut:
        for j, field in enumerate(total):
            for q in range(4):
                outs[0][j, q] = field[q]
        return
    mine, others = outs
    others[...] = jnp.zeros_like(others)
    rows = mine.shape[2]
    parts = edge // rows
    for k in range(parts):
        group = wide(own[1:2], rows, home[0][0].shape[1]) + k
        group = jnp.where(group >= parts, group - parts, group)
        for j, field in enumerate(total):
            cuts = [[q[p * rows : (p + 1) * rows] for q in field] for p in range(parts)]
            for q, piece in enumerate(choose(cuts, group)):
                if k == 0:
                    mine[j, q] = piece
                else:
                    others[k - 1, (4 * j + q) * rows : (4 * j + q + 1) * rows, :] = piece


def gate_kernel(_, out):
    out[...] = jnp.zeros_like(out)


def sum_kernel(number, *refs):
    parts, (table, terms, trav_total, res_total) = refs[:number], refs[number:]
    fields = [[terms[j, q] for q in range(4)] for j in range(terms.shape[0])]
    for j, field in enumerate(unfold(fields, table[...])):
        res_total[j] = field
    total = []
    size = parts[0].shape[2]
    for j in range(parts[0].shape[0]):
        starts = [(4 * j + q) * size for q in range(4)]
        total.append([sum((part[k : k + size, :] for part in parts[1:]), parts[0][j, q]) for q, k in enumerate(starts)])
    for j, field in enumerate(unfold(total, table[...])):
        trav_total[j] = field


VMEM = pl.BlockSpec(memory_space=pltpu.VMEM)
HBM = pl.BlockSpec(memory_space=pl.ANY)
LIMIT = pltpu.CompilerParams(vmem_limit_bytes=32 * 1024 * 1024)
LIMIT_U = pltpu.CompilerParams(vmem_limit_bytes=60 * 1024 * 1024)
LIMIT_W = pltpu.CompilerParams(vmem_limit_bytes=32 * 1024 * 1024)


def cost(microseconds):
    return pl.CostEstimate(flops=int(microseconds * 1e9), bytes_accessed=1024, transcendentals=0)


def from_behind(value, by):
    peers = lax.axis_size("blk")
    return lax.ppermute(value, "blk", [(i, (i + by) % peers) for i in range(peers)])


def other_core(value):
    peers = lax.axis_size("blk")
    return lax.ppermute(value, "blk", [(i, i ^ 1) for i in range(peers)])


def local(residents, travellers, pair_list):
    count, edge, plane = residents.shape
    held = travellers.shape[0]
    steps, slots = pair_list.shape[1:3]
    direct = range(2, steps + 1, 2)
    arrivals = len(direct)
    groups = lax.axis_size("grp")
    part = edge // groups
    fields = 2 * slots
    small = jnp.asarray(small_tables(edge, fields))

    shape = (8 * count * edge + info_rows(steps, slots), plane // 8)
    packed = pl.pallas_call(
        functools.partial(pack_kernel, ("blk", "grp")),
        out_shape=jax.ShapeDtypeStruct(shape, jnp.bfloat16),
        in_specs=[HBM, HBM],
        out_specs=HBM,
        scratch_shapes=[
            pltpu.VMEM(residents.shape, jnp.bfloat16),
            pltpu.SMEM((1, 3, slots, steps), jnp.int32),
            pltpu.VMEM(shape, jnp.bfloat16),
            pltpu.SemaphoreType.DMA((2 + count,)),
        ],
        compiler_params=LIMIT_U,
        cost_estimate=cost(1),
        name="pack",
    )(residents, jnp.transpose(pair_list, (0, 3, 2, 1)))
    *tables, folding, unfolding, moving = pl.pallas_call(
        functools.partial(tables_kernel, fields),
        out_shape=(
            jax.ShapeDtypeStruct((plane // 2, plane // 4), jnp.bfloat16),
            jax.ShapeDtypeStruct((2 * fields * edge, fields * edge), jnp.bfloat16),
            jax.ShapeDtypeStruct((edge, plane), jnp.float32),
            jax.ShapeDtypeStruct((plane // 2, plane // 2), jnp.bfloat16),
            jax.ShapeDtypeStruct((plane // 2, plane // 2), jnp.bfloat16),
            jax.ShapeDtypeStruct((8 * held * edge, plane // 8), jnp.bfloat16),
        ),
        in_specs=[VMEM, VMEM],
        out_specs=(VMEM,) * 6,
        compiler_params=LIMIT,
        cost_estimate=cost(20),
        name="tables",
    )(small, travellers)

    def stage(plan, blocks, home, total, for_travellers, microseconds, name, cut=False, after=()):
        number = home[1].shape[0] // (8 * edge)
        if cut:
            out_shape = (
                jax.ShapeDtypeStruct((number, 4, part, plane // 4), jnp.float32),
                jax.ShapeDtypeStruct((groups - 1, number * 4 * part + SPARE_ROWS, plane // 4), jnp.float32),
            )
        else:
            out_shape = jax.ShapeDtypeStruct((number, 4, edge, plane // 4), jnp.float32)
        operands = (*blocks, *home, *tables, folding) + (() if total is None else (total,))
        return pl.pallas_call(
            functools.partial(
                terms_kernel, plan, total is not None, cut, slots, edge, for_travellers, len(after)
            ),
            out_shape=out_shape,
            in_specs=[VMEM] * (len(operands) + len(after)),
            out_specs=jax.tree.map(lambda _: VMEM, out_shape),
            compiler_params=LIMIT,
            cost_estimate=cost(microseconds),
            name=name,
        )(*operands, *after)

    last = arrivals - 1

    def straight(k):
        return 1, (2 * k + 1, 2 * k + 1)

    middle = [(1, (2 * k + 2, 2 * k)) for k in range(last)]
    ends = [(2, (0, 2 * last))]

    res_moved = [from_behind(packed, -s) for s in direct]
    res_moved[last], own, moving = lax.optimization_barrier((res_moved[last], packed, moving))
    res_swapped = [other_core(own)] + [other_core(value) for value in res_moved]
    passed, packed_first = lax.optimization_barrier((travellers, packed))
    trav_moved = [from_behind(passed, s) for s in direct]
    trav_swapped = [other_core(passed)]

    def gate(value, microseconds):
        return pl.pallas_call(
            gate_kernel,
            out_shape=jax.ShapeDtypeStruct((8, 128), jnp.float32),
            in_specs=[HBM],
            out_specs=VMEM,
            compiler_params=LIMIT,
            cost_estimate=cost(microseconds),
            name="gate",
        )(value)

    arrived = gate(res_moved[0], 20)

    home = (packed, moving)
    total = stage([straight(last)], [res_moved[last]], home, None, True, 10, "first_traveller_terms")
    blocks = [res_swapped[0], res_swapped[-1]]
    total = stage(ends, blocks, home, total, True, 10, "early_traveller_terms")
    for k in range(last):
        res_moved[k], total = lax.optimization_barrier((res_moved[k], total))
        total = stage([straight(k)], [res_moved[k]], home, total, True, 1, "middle_traveller_terms")
    blocks = [other_core(value) for value in res_moved[:last]]
    mine, others = stage(middle, blocks, home, total, True, 2, "late_traveller_terms", cut=True, after=(arrived,))

    summed = gate(others, 1)
    trav_moved, summed = lax.optimization_barrier((trav_moved, summed))
    trav_swapped += [other_core(value) for value in trav_moved]
    sent = [
        lax.ppermute(others[k - 1], "grp", [(g, (g + k) % groups) for g in range(groups)])
        for k in range(1, groups)
    ]
    home = (packed, packed)
    total = stage(
        [straight(k) for k in range(arrivals)],
        trav_moved,
        home,
        None,
        False,
        0.001,
        "early_resident_terms",
        after=(summed,),
    )
    blocks = [*trav_swapped[1:-1], trav_swapped[0], trav_swapped[-1]]
    res_total = stage(middle + ends, blocks, home, total, False, 0.001, "late_resident_terms")
    res_total, sent = lax.optimization_barrier((res_total, sent))
    parts = [mine, *sent]
    trav_total, res_total = pl.pallas_call(
        functools.partial(sum_kernel, len(parts)),
        out_shape=(
            jax.ShapeDtypeStruct((held, part, plane), jnp.float32),
            jax.ShapeDtypeStruct(residents.shape, jnp.float32),
        ),
        in_specs=[VMEM] * (len(parts) + 2),
        out_specs=(VMEM, VMEM),
        compiler_params=LIMIT,
        cost_estimate=cost(0.5),
        name="sums",
    )(*parts, unfolding, res_total)
    return res_total, trav_total


def solution(mesh):
    return jax.shard_map(
        local,
        mesh=mesh,
        in_specs=(
            P(("blk", "grp"), None, None),
            P("blk", None, None),
            P(("blk", "grp"), None, None, None),
        ),
        out_specs=(P(("blk", "grp"), None, None), P("blk", "grp", None)),
        check_vma=False,
    )
```

```python
import functools

import jax
import jax.numpy as jnp
import numpy as np
from jax import lax
from jax.experimental import pallas as pl
from jax.experimental.pallas import tpu as pltpu
from jax.sharding import PartitionSpec as P


SPARE_ROWS = 8
LANES = 128


@functools.lru_cache
def small_tables(edge, fields):
    index = np.arange(edge) + 1.0
    sine = np.sqrt(2.0 / (edge + 1)) * np.sin(np.pi * np.outer(index, index) / (edge + 1))
    eigen = 2.0 - 2.0 * np.cos(np.pi * index / (edge + 1))
    part = sine[::2, ::2]
    split = (eigen[::2], eigen[::-1][::2])
    plane = [np.add.outer(split[b], split[c]).reshape(-1) for b in (0, 1) for c in (0, 1)]
    lanes = max(edge * edge // 4, 2 * fields * edge)
    rows = [
        np.repeat(part, edge // 2, axis=1),
        np.tile(part, (1, edge // 2)),
        np.concatenate([np.tile(sine, (1, fields)), np.tile(eigen[:, None], (1, fields * edge))], axis=1),
        np.stack(plane),
        np.zeros((4, 1)),
    ]
    return np.concatenate([np.pad(r, ((0, 0), (0, lanes - r.shape[1]))) for r in rows]).astype(np.float32)


def make_tables(small, edge, fields, plane_table, along, inverse):
    part, lanes, rows = edge // 2, edge * edge // 4, fields * edge
    second = small[part : 2 * part, :lanes]
    for n in range(part):
        high, low = halves(small[n : n + 1, :lanes] * second)
        plane_table[n * part : (n + 1) * part, :] = high
        plane_table[lanes + n * part : lanes + (n + 1) * part, :] = low
    sine = jnp.concatenate([small[edge : 2 * edge, :rows]] * fields, axis=0)
    row = lax.broadcasted_iota(jnp.int32, (rows, rows), 0)
    column = lax.broadcasted_iota(jnp.int32, (rows, rows), 1)
    high, low = halves(jnp.where(row // edge == column // edge, sine, 0.0))
    along[:rows, :] = high
    along[rows:, :] = low
    eigen = small[edge : 2 * edge, rows : rows + 1]
    for q in range(4):
        plane = small[2 * edge + q : 2 * edge + q + 1, :lanes]
        inverse[:, q * lanes : (q + 1) * lanes] = 1.0 / (eigen + plane)


def fold_source(lane, edge):
    small = edge // 2
    point_c = lane % small
    point_b = (lane // small) % (edge // 4)
    quadrant = lane // (small * (edge // 4))
    b = jnp.where(quadrant < 2, 2 * point_b, small - 1 - 2 * point_b)
    c = jnp.where(quadrant % 2 == 0, 2 * point_c, edge - 1 - 2 * point_c)
    return b * edge + c


def fold_table(edge, transposed):
    lanes = edge * edge // 2
    dim = 0 if transposed else 1
    folded = fold_source(lax.broadcasted_iota(jnp.int32, (lanes, 1) if transposed else (1, lanes), dim), edge)
    plain = lax.broadcasted_iota(jnp.int32, (lanes, lanes), 1 - dim)
    return jnp.where(plain == folded, 1.0, 0.0).astype(jnp.bfloat16)


def tile_of(quadrant, half):
    return 2 * quadrant + (half if quadrant < 2 else 1 - half)


def dot(x, y):
    return jnp.dot(x, y, preferred_element_type=jnp.float32)


def halves(x):
    high = x.astype(jnp.bfloat16)
    return high, (x - high.astype(jnp.float32)).astype(jnp.bfloat16)


def times_table(x, table):
    high, low = table[: table.shape[0] // 2], table[table.shape[0] // 2 :]
    parts = []
    for start in range(0, x.shape[0], LANES):
        x_high, x_low = halves(x[start : start + LANES])
        parts.append(dot(x_high, high) + (dot(x_low, high) + dot(x_high, low)))
    return jnp.concatenate(parts, axis=0)


def table_times(table, x):
    high, low = table[: table.shape[0] // 2], table[table.shape[0] // 2 :]
    table = jnp.concatenate([high, high, low], axis=1)
    parts = []
    for start in range(0, x.shape[1], 2 * LANES):
        x_high, x_low = halves(x[:, start : start + 2 * LANES])
        parts.append(dot(table, jnp.concatenate([x_high, x_low, x_high], axis=0)))
    return jnp.concatenate(parts, axis=1)


def spread(quadrants):
    a, b, c, d = quadrants
    return [a + b + (c + d), a - b + (c - d), a + b - (c + d), a - b - (c - d)]


def info_rows(steps, slots):
    return -(-(steps * slots * 3 + 2) // 16) * 16


def store_folded(fields, table, target):
    count, edge, plane = fields.shape
    half, lanes = plane // 2, plane // 8
    rows = [fields[i, :, h * half : (h + 1) * half] for i in range(count) for h in (0, 1)]
    folded = dot(jnp.concatenate(rows, axis=0), table).astype(jnp.bfloat16)
    for i in range(count):
        for h in (0, 1):
            start = (2 * i + h) * edge
            for q in range(4):
                row = (tile_of(q, h) * count + i) * edge
                target[row : row + edge, :] = folded[start : start + edge, q * lanes : (q + 1) * lanes]


def pack_kernel(axes, residents, pairs, packed, fields, entries_ref, folded, sems):
    count, edge, plane = residents.shape
    loads = [pltpu.make_async_copy(residents.at[i], fields.at[i], sems.at[2 + i]) for i in range(count)]
    load_entries = pltpu.make_async_copy(pairs, entries_ref, sems.at[1])
    for load in loads:
        load.start()
    load_entries.start()
    table = fold_table(edge, False)
    load_entries.wait()
    _, entries, slots, steps = pairs.shape
    row = lax.broadcasted_iota(jnp.int32, (info_rows(steps, slots), packed.shape[1]), 0)
    values = jnp.zeros(row.shape, jnp.int32)
    scalars = [entries_ref[0, e, p, s] for s in range(steps) for p in range(slots) for e in range(entries)]
    for k, value in enumerate([lax.axis_index(axes[0]) % 2, lax.axis_index(axes[1]), *scalars]):
        values = jnp.where(row == k, value, values)
    folded[8 * count * edge :, :] = values.astype(jnp.float32).astype(jnp.bfloat16)
    for load in loads:
        load.wait()
    store_folded(fields, table, folded)
    store = pltpu.make_async_copy(folded, packed, sems.at[0])
    store.start()
    store.wait()


def tables_kernel(count, small, travellers, plane_table, along, inverse, folding, unfolding, moving):
    edge = inverse.shape[0]
    make_tables(small, edge, count, plane_table, along, inverse)
    folding[...] = fold_table(edge, False)
    unfolding[...] = fold_table(edge, True)
    store_folded(travellers, folding[...], moving)


class Fields:
    def __init__(self, count, edge, *refs, near=None):
        self.count, self.edge, self.refs, self.near = count, edge, refs, near

    def rows(self, start, size):
        values = [ref[start : start + size, :].astype(jnp.float32) for ref in self.refs]
        return jnp.where(self.near, *values) if len(values) == 2 else values[0]

    def quadrants(self, i):
        tiles = [self.rows((t * self.count + i) * self.edge, self.edge) for t in range(8)]
        return [jnp.concatenate(tiles[2 * q : 2 * q + 2], axis=1) for q in range(4)]

    def info(self, count=None):
        start = 8 * self.count * self.edge
        return self.rows(start, self.refs[0].shape[0] - start)


class PlainFields:
    def __init__(self, count, edge, *refs, near=None, table=None):
        self.count, self.edge, self.near = count, edge, near
        half = edge * edge // 2
        values = [[ref[i].astype(jnp.float32) for i in range(count)] for ref in refs]
        fields = values[0]
        if len(values) == 2:
            fields = [jnp.where(near, *pair) for pair in zip(*values)]
        rows = [field[:, h * half : (h + 1) * half] for field in fields for h in (0, 1)]
        self.folded = dot(jnp.concatenate(rows, axis=0).astype(jnp.bfloat16), table)

    def quadrants(self, i):
        edge, lanes = self.edge, self.folded.shape[1] // 4
        found = []
        for q in range(4):
            order = (0, 1) if q < 2 else (1, 0)
            tiles = [
                self.folded[(2 * i + h) * edge : (2 * i + h + 1) * edge, q * lanes : (q + 1) * lanes]
                for h in order
            ]
            found.append(jnp.concatenate(tiles, axis=1))
        return found


def wide(row, edge, lanes):
    return jnp.broadcast_to(jnp.concatenate([row] * (lanes // row.shape[1]), axis=1), (edge, lanes))


def choose(fields, index):
    chosen = fields[0]
    for i in range(1, len(fields)):
        chosen = [jnp.where(index == i, new, old) for new, old in zip(fields[i], chosen)]
    return chosen


def slot_rows(info, arrival, slots):
    start = 2 + arrival * slots * 3
    return [info[start + 3 * p : start + 3 * p + 3] for p in range(slots)]


def gather_terms(slots, home, total, tables):
    plane_table, along, inverse = (table[...] for table in tables)
    edge = inverse.shape[0]
    rows = len(slots) * edge
    densities = []
    for moving, index, _ in slots:
        densities.append(spread([m * h for m, h in zip(moving, choose(home, index))]))
    field = jnp.concatenate([density[q] for q in range(4) for density in densities], axis=0)
    field = times_table(field, plane_table)
    field = jnp.concatenate([field[q * rows : (q + 1) * rows] for q in range(4)], axis=1)
    size = along.shape[0] // 2
    along = jnp.concatenate([along[:rows, :rows], along[size : size + rows, :rows]], axis=0)
    field = table_times(along, field)
    field = (field.reshape(len(slots), edge, -1) * inverse[None]).reshape(field.shape)
    field = table_times(along, field)
    lanes = field.shape[1] // 4
    field = jnp.concatenate([field[:, q * lanes : (q + 1) * lanes] for q in range(4)], axis=0)
    field = times_table(field, plane_table)
    for slot, (moving, index, active) in enumerate(slots):
        potential = spread([field[q * rows + slot * edge : q * rows + (slot + 1) * edge] for q in range(4)])
        terms = [active * p * m for p, m in zip(potential, moving)]
        for j in range(len(home)):
            total[j] = [old + jnp.where(index == j, new, 0.0) for old, new in zip(total[j], terms)]


def zero_total(home):
    return [[jnp.zeros_like(q) for q in field] for field in home]


def unfold(fields, table):
    rows = fields[0][0].shape[0]
    lanes = table.shape[0] // 4
    stack = []
    for field in fields:
        for h in (0, 1):
            tiles = [tile_of(q, h) for q in range(4)]
            stack.append(
                jnp.concatenate(
                    [field[t // 2][:, (t % 2) * lanes : (t % 2 + 1) * lanes] for t in tiles], axis=1
                )
            )
    high, low = halves(jnp.concatenate(stack, axis=0))
    plain = dot(high, table) + dot(low, table)
    return [
        jnp.concatenate([plain[k * rows : (k + 1) * rows] for k in (2 * i, 2 * i + 1)], axis=1)
        for i in range(len(fields))
    ]


def slots_of(block, info, near, arrivals, slots, entry):
    edge = block.edge
    fields = [block.quadrants(i) for i in range(block.count)]
    lanes = fields[0][0].shape[1]
    found = []
    for row, far in zip(slot_rows(info, arrivals[0], slots), slot_rows(info, arrivals[1], slots)):
        row = jnp.where(near, row, far)
        own, other, active = (wide(row[e : e + 1], edge, lanes) for e in (entry, 1 - entry, 2))
        found.append((choose(fields, own), other, active))
    return found


def terms_kernel(plan, accumulate, cut, plain, slots, edge, for_travellers, after, *refs):
    outputs = 2 if cut else 1
    refs, outs = refs[:-outputs], refs[-outputs:]
    refs, others = refs[: len(refs) - after], refs[len(refs) - after :]
    blocks = sum(number for number, _ in plan)
    moving, (own, home, *refs) = refs[:blocks], refs[blocks:]
    tables, folding, before = refs[:3], refs[3], refs[4:]
    held = home.shape[0] // (8 * edge)
    count = moving[0].shape[0] // (8 * edge) if for_travellers else moving[0].shape[0]
    own = Fields(own.shape[0] // (8 * edge), edge, own).info()
    near = own[0:1] == (0 if for_travellers else 1)
    home = Fields(held, edge, home)
    home = [home.quadrants(j) for j in range(held)]
    found = []
    for number, arrivals in plan:
        sources, moving = moving[:number], moving[number:]
        if for_travellers:
            block = Fields(count, edge, *sources, near=near)
        else:
            block = PlainFields(count, edge, *sources, near=near[0:1, 0:1], table=folding[...])
        info = block.info() if for_travellers else own
        found += slots_of(block, info, near, arrivals, slots, 0 if for_travellers else 1)
    total = [[before[0][j, q] for q in range(4)] for j in range(held)] if accumulate else zero_total(home)
    group = 2 * slots
    for start in range(0, len(found), group):
        gather_terms(found[start : start + group], home, total, tables)
    if plain:
        for j, field in enumerate(unfold(total, others[0][...])):
            outs[0][j] = field
        return
    if not cut:
        for j, field in enumerate(total):
            for q in range(4):
                outs[0][j, q] = field[q]
        return
    mine, others = outs
    others[...] = jnp.zeros_like(others)
    rows = mine.shape[2]
    parts = edge // rows
    for k in range(parts):
        group = wide(own[1:2], rows, home[0][0].shape[1]) + k
        group = jnp.where(group >= parts, group - parts, group)
        for j, field in enumerate(total):
            cuts = [[q[p * rows : (p + 1) * rows] for q in field] for p in range(parts)]
            for q, piece in enumerate(choose(cuts, group)):
                if k == 0:
                    mine[j, q] = piece
                else:
                    others[k - 1, (4 * j + q) * rows : (4 * j + q + 1) * rows, :] = piece


def gate_kernel(_, out):
    out[...] = jnp.zeros_like(out)


def sum_kernel(number, *refs):
    parts, (table, terms, trav_out, res_out, trav_total, sems) = refs[:number], refs[number:]
    copies = [pltpu.make_async_copy(terms, res_out, sems.at[0])]
    copies[0].start()
    total = []
    size = parts[0].shape[2]
    for j in range(parts[0].shape[0]):
        starts = [(4 * j + q) * size for q in range(4)]
        total.append([sum((part[k : k + size, :] for part in parts[1:]), parts[0][j, q]) for q, k in enumerate(starts)])
    for j, field in enumerate(unfold(total, table[...])):
        trav_total[j] = field
    copies.append(pltpu.make_async_copy(trav_total, trav_out, sems.at[1]))
    copies[-1].start()
    for copy in copies:
        copy.wait()


VMEM = pl.BlockSpec(memory_space=pltpu.VMEM)
HBM = pl.BlockSpec(memory_space=pl.ANY)
LIMIT = pltpu.CompilerParams(vmem_limit_bytes=32 * 1024 * 1024)
LIMIT_U = pltpu.CompilerParams(vmem_limit_bytes=60 * 1024 * 1024)
LIMIT_W = pltpu.CompilerParams(vmem_limit_bytes=32 * 1024 * 1024)


def cost(microseconds):
    return pl.CostEstimate(flops=int(microseconds * 1e9), bytes_accessed=1024, transcendentals=0)


def from_behind(value, by):
    peers = lax.axis_size("blk")
    return lax.ppermute(value, "blk", [(i, (i + by) % peers) for i in range(peers)])


def other_core(value):
    peers = lax.axis_size("blk")
    return lax.ppermute(value, "blk", [(i, i ^ 1) for i in range(peers)])


def local(residents, travellers, pair_list):
    count, edge, plane = residents.shape
    held = travellers.shape[0]
    steps, slots = pair_list.shape[1:3]
    direct = range(2, steps + 1, 2)
    arrivals = len(direct)
    groups = lax.axis_size("grp")
    part = edge // groups
    fields = 2 * slots
    small = jnp.asarray(small_tables(edge, fields))

    shape = (8 * count * edge + info_rows(steps, slots), plane // 8)
    packed = pl.pallas_call(
        functools.partial(pack_kernel, ("blk", "grp")),
        out_shape=jax.ShapeDtypeStruct(shape, jnp.bfloat16),
        in_specs=[HBM, HBM],
        out_specs=HBM,
        scratch_shapes=[
            pltpu.VMEM(residents.shape, jnp.bfloat16),
            pltpu.SMEM((1, 3, slots, steps), jnp.int32),
            pltpu.VMEM(shape, jnp.bfloat16),
            pltpu.SemaphoreType.DMA((2 + count,)),
        ],
        compiler_params=LIMIT_U,
        cost_estimate=cost(1),
        name="pack",
    )(residents, jnp.transpose(pair_list, (0, 3, 2, 1)))
    *tables, folding, unfolding, moving = pl.pallas_call(
        functools.partial(tables_kernel, fields),
        out_shape=(
            jax.ShapeDtypeStruct((plane // 2, plane // 4), jnp.bfloat16),
            jax.ShapeDtypeStruct((2 * fields * edge, fields * edge), jnp.bfloat16),
            jax.ShapeDtypeStruct((edge, plane), jnp.float32),
            jax.ShapeDtypeStruct((plane // 2, plane // 2), jnp.bfloat16),
            jax.ShapeDtypeStruct((plane // 2, plane // 2), jnp.bfloat16),
            jax.ShapeDtypeStruct((8 * held * edge, plane // 8), jnp.bfloat16),
        ),
        in_specs=[VMEM, VMEM],
        out_specs=(VMEM,) * 6,
        compiler_params=LIMIT,
        cost_estimate=cost(20),
        name="tables",
    )(small, travellers)

    def stage(plan, blocks, home, total, for_travellers, microseconds, name, cut=False, plain=False, after=()):
        number = home[1].shape[0] // (8 * edge)
        if cut:
            out_shape = (
                jax.ShapeDtypeStruct((number, 4, part, plane // 4), jnp.float32),
                jax.ShapeDtypeStruct((groups - 1, number * 4 * part + SPARE_ROWS, plane // 4), jnp.float32),
            )
        elif plain:
            out_shape = jax.ShapeDtypeStruct((number, edge, plane), jnp.float32)
        else:
            out_shape = jax.ShapeDtypeStruct((number, 4, edge, plane // 4), jnp.float32)
        operands = (*blocks, *home, *tables, folding) + (() if total is None else (total,))
        return pl.pallas_call(
            functools.partial(
                terms_kernel, plan, total is not None, cut, plain, slots, edge, for_travellers, len(after)
            ),
            out_shape=out_shape,
            in_specs=[VMEM] * (len(operands) + len(after)),
            out_specs=jax.tree.map(lambda _: VMEM, out_shape),
            compiler_params=LIMIT,
            cost_estimate=cost(microseconds),
            name=name,
        )(*operands, *after)

    last = arrivals - 1

    def straight(k):
        return 1, (2 * k + 1, 2 * k + 1)

    middle = [(1, (2 * k + 2, 2 * k)) for k in range(last)]
    ends = [(2, (0, 2 * last))]

    res_moved = [from_behind(packed, -s) for s in direct]
    res_moved[last], own, moving = lax.optimization_barrier((res_moved[last], packed, moving))
    res_swapped = [other_core(own)] + [other_core(value) for value in res_moved]
    passed, packed_first = lax.optimization_barrier((travellers, packed))
    trav_moved = [from_behind(passed, s) for s in direct]
    trav_swapped = [other_core(passed)]

    def gate(value, microseconds):
        return pl.pallas_call(
            gate_kernel,
            out_shape=jax.ShapeDtypeStruct((8, 128), jnp.float32),
            in_specs=[HBM],
            out_specs=VMEM,
            compiler_params=LIMIT,
            cost_estimate=cost(microseconds),
            name="gate",
        )(value)

    arrived = gate(res_moved[0], 20)

    home = (packed, moving)
    total = stage([straight(last)], [res_moved[last]], home, None, True, 10, "first_traveller_terms")
    blocks = [res_swapped[0], res_swapped[-1]]
    total = stage(ends, blocks, home, total, True, 10, "early_traveller_terms")
    for k in range(last):
        res_moved[k], total = lax.optimization_barrier((res_moved[k], total))
        total = stage([straight(k)], [res_moved[k]], home, total, True, 1, "middle_traveller_terms")
    blocks = [other_core(value) for value in res_moved[:last]]
    mine, others = stage(middle, blocks, home, total, True, 2, "late_traveller_terms", cut=True, after=(arrived,))

    summed = gate(others, 1)
    trav_moved, summed = lax.optimization_barrier((trav_moved, summed))
    trav_swapped += [other_core(value) for value in trav_moved]
    sent = [
        lax.ppermute(others[k - 1], "grp", [(g, (g + k) % groups) for g in range(groups)])
        for k in range(1, groups)
    ]
    home = (packed, packed)
    total = stage(
        [straight(k) for k in range(arrivals)],
        trav_moved,
        home,
        None,
        False,
        0.001,
        "early_resident_terms",
        after=(summed,),
    )
    blocks = [*trav_swapped[1:-1], trav_swapped[0], trav_swapped[-1]]
    res_total = stage(middle + ends, blocks, home, total, False, 0.001, "late_resident_terms", plain=True, after=(unfolding,))
    res_total, sent = lax.optimization_barrier((res_total, sent))
    parts = [mine, *sent]
    trav_total, res_total = pl.pallas_call(
        functools.partial(sum_kernel, len(parts)),
        out_shape=(
            jax.ShapeDtypeStruct((held, part, plane), jnp.float32),
            jax.ShapeDtypeStruct(residents.shape, jnp.float32),
        ),
        in_specs=[VMEM] * (len(parts) + 2),
        out_specs=(HBM, HBM),
        scratch_shapes=[
            pltpu.VMEM((held, part, plane), jnp.float32),
            pltpu.SemaphoreType.DMA((2,)),
        ],
        compiler_params=LIMIT,
        cost_estimate=cost(0.5),
        name="sums",
    )(*parts, unfolding, res_total)
    return res_total, trav_total


def solution(mesh):
    return jax.shard_map(
        local,
        mesh=mesh,
        in_specs=(
            P(("blk", "grp"), None, None),
            P("blk", None, None),
            P(("blk", "grp"), None, None, None),
        ),
        out_specs=(P(("blk", "grp"), None, None), P("blk", "grp", None)),
        check_vma=False,
    )
```

```python
import functools

import jax
import jax.numpy as jnp
import numpy as np
from jax import lax
from jax.experimental import pallas as pl
from jax.experimental.pallas import tpu as pltpu
from jax.sharding import PartitionSpec as P


SPARE_ROWS = 8
LANES = 128


@functools.lru_cache
def small_tables(edge, fields):
    index = np.arange(edge) + 1.0
    sine = np.sqrt(2.0 / (edge + 1)) * np.sin(np.pi * np.outer(index, index) / (edge + 1))
    eigen = 2.0 - 2.0 * np.cos(np.pi * index / (edge + 1))
    part = sine[::2, ::2]
    split = (eigen[::2], eigen[::-1][::2])
    plane = [np.add.outer(split[b], split[c]).reshape(-1) for b in (0, 1) for c in (0, 1)]
    lanes = max(edge * edge // 4, 2 * fields * edge)
    rows = [
        np.repeat(part, edge // 2, axis=1),
        np.tile(part, (1, edge // 2)),
        np.concatenate([np.tile(sine, (1, fields)), np.tile(eigen[:, None], (1, fields * edge))], axis=1),
        np.stack(plane),
        np.zeros((4, 1)),
    ]
    return np.concatenate([np.pad(r, ((0, 0), (0, lanes - r.shape[1]))) for r in rows]).astype(np.float32)


def make_tables(small, edge, fields, plane_table, along, inverse):
    part, lanes, rows = edge // 2, edge * edge // 4, fields * edge
    second = small[part : 2 * part, :lanes]
    for n in range(part):
        high, low = halves(small[n : n + 1, :lanes] * second)
        plane_table[n * part : (n + 1) * part, :] = high
        plane_table[lanes + n * part : lanes + (n + 1) * part, :] = low
    sine = jnp.concatenate([small[edge : 2 * edge, :rows]] * fields, axis=0)
    row = lax.broadcasted_iota(jnp.int32, (rows, rows), 0)
    column = lax.broadcasted_iota(jnp.int32, (rows, rows), 1)
    high, low = halves(jnp.where(row // edge == column // edge, sine, 0.0))
    along[:rows, :] = high
    along[rows:, :] = low
    eigen = small[edge : 2 * edge, rows : rows + 1]
    for q in range(4):
        plane = small[2 * edge + q : 2 * edge + q + 1, :lanes]
        inverse[:, q * lanes : (q + 1) * lanes] = 1.0 / (eigen + plane)


def fold_source(lane, edge):
    small = edge // 2
    point_c = lane % small
    point_b = (lane // small) % (edge // 4)
    quadrant = lane // (small * (edge // 4))
    b = jnp.where(quadrant < 2, 2 * point_b, small - 1 - 2 * point_b)
    c = jnp.where(quadrant % 2 == 0, 2 * point_c, edge - 1 - 2 * point_c)
    return b * edge + c


def fold_table(edge, transposed):
    lanes = edge * edge // 2
    dim = 0 if transposed else 1
    folded = fold_source(lax.broadcasted_iota(jnp.int32, (lanes, 1) if transposed else (1, lanes), dim), edge)
    plain = lax.broadcasted_iota(jnp.int32, (lanes, lanes), 1 - dim)
    return jnp.where(plain == folded, 1.0, 0.0).astype(jnp.bfloat16)


def tile_of(quadrant, half):
    return 2 * quadrant + (half if quadrant < 2 else 1 - half)


def dot(x, y):
    return jnp.dot(x, y, preferred_element_type=jnp.float32)


def halves(x):
    high = x.astype(jnp.bfloat16)
    return high, (x - high.astype(jnp.float32)).astype(jnp.bfloat16)


def times_table(x, table):
    high, low = table[: table.shape[0] // 2], table[table.shape[0] // 2 :]
    parts = []
    for start in range(0, x.shape[0], LANES):
        x_high, x_low = halves(x[start : start + LANES])
        parts.append(dot(x_high, high) + (dot(x_low, high) + dot(x_high, low)))
    return jnp.concatenate(parts, axis=0)


def table_times(table, x):
    high, low = table[: table.shape[0] // 2], table[table.shape[0] // 2 :]
    table = jnp.concatenate([high, high, low], axis=1)
    parts = []
    for start in range(0, x.shape[1], 2 * LANES):
        x_high, x_low = halves(x[:, start : start + 2 * LANES])
        parts.append(dot(table, jnp.concatenate([x_high, x_low, x_high], axis=0)))
    return jnp.concatenate(parts, axis=1)


def spread(quadrants):
    a, b, c, d = quadrants
    return [a + b + (c + d), a - b + (c - d), a + b - (c + d), a - b - (c - d)]


def info_rows(steps, slots):
    return -(-(steps * slots * 3 + 2) // 16) * 16


def store_folded(fields, table, target):
    count, edge, plane = fields.shape
    half, lanes = plane // 2, plane // 8
    rows = [fields[i, :, h * half : (h + 1) * half] for i in range(count) for h in (0, 1)]
    folded = dot(jnp.concatenate(rows, axis=0), table).astype(jnp.bfloat16)
    for i in range(count):
        for h in (0, 1):
            start = (2 * i + h) * edge
            for q in range(4):
                row = (tile_of(q, h) * count + i) * edge
                target[row : row + edge, :] = folded[start : start + edge, q * lanes : (q + 1) * lanes]


def pack_kernel(axes, residents, pairs, packed, fields, entries_ref, folded, sems):
    count, edge, plane = residents.shape
    loads = [pltpu.make_async_copy(residents.at[i], fields.at[i], sems.at[2 + i]) for i in range(count)]
    load_entries = pltpu.make_async_copy(pairs, entries_ref, sems.at[1])
    for load in loads:
        load.start()
    load_entries.start()
    table = fold_table(edge, False)
    load_entries.wait()
    _, entries, slots, steps = pairs.shape
    row = lax.broadcasted_iota(jnp.int32, (info_rows(steps, slots), packed.shape[1]), 0)
    values = jnp.zeros(row.shape, jnp.int32)
    scalars = [entries_ref[0, e, p, s] for s in range(steps) for p in range(slots) for e in range(entries)]
    for k, value in enumerate([lax.axis_index(axes[0]) % 2, lax.axis_index(axes[1]), *scalars]):
        values = jnp.where(row == k, value, values)
    folded[8 * count * edge :, :] = values.astype(jnp.float32).astype(jnp.bfloat16)
    for load in loads:
        load.wait()
    store_folded(fields, table, folded)
    cut = 4 * count * edge
    stores = [
        pltpu.make_async_copy(folded.at[:cut], packed.at[:cut], sems.at[0]),
        pltpu.make_async_copy(folded.at[cut:], packed.at[cut:], sems.at[1]),
    ]
    for store in stores:
        store.start()
    for store in stores:
        store.wait()


def tables_kernel(count, small, travellers, plane_table, along, inverse, folding, unfolding, moving):
    edge = inverse.shape[0]
    make_tables(small, edge, count, plane_table, along, inverse)
    folding[...] = fold_table(edge, False)
    unfolding[...] = fold_table(edge, True)
    store_folded(travellers, folding[...], moving)


class Fields:
    def __init__(self, count, edge, *refs, near=None):
        self.count, self.edge, self.refs, self.near = count, edge, refs, near

    def rows(self, start, size):
        values = [ref[start : start + size, :].astype(jnp.float32) for ref in self.refs]
        return jnp.where(self.near, *values) if len(values) == 2 else values[0]

    def quadrants(self, i):
        tiles = [self.rows((t * self.count + i) * self.edge, self.edge) for t in range(8)]
        return [jnp.concatenate(tiles[2 * q : 2 * q + 2], axis=1) for q in range(4)]

    def info(self, count=None):
        start = 8 * self.count * self.edge
        return self.rows(start, self.refs[0].shape[0] - start)


class PlainFields:
    def __init__(self, count, edge, *refs, near=None, table=None):
        self.count, self.edge, self.near = count, edge, near
        half = edge * edge // 2
        values = [[ref[i].astype(jnp.float32) for i in range(count)] for ref in refs]
        fields = values[0]
        if len(values) == 2:
            fields = [jnp.where(near, *pair) for pair in zip(*values)]
        rows = [field[:, h * half : (h + 1) * half] for field in fields for h in (0, 1)]
        self.folded = dot(jnp.concatenate(rows, axis=0).astype(jnp.bfloat16), table)

    def quadrants(self, i):
        edge, lanes = self.edge, self.folded.shape[1] // 4
        found = []
        for q in range(4):
            order = (0, 1) if q < 2 else (1, 0)
            tiles = [
                self.folded[(2 * i + h) * edge : (2 * i + h + 1) * edge, q * lanes : (q + 1) * lanes]
                for h in order
            ]
            found.append(jnp.concatenate(tiles, axis=1))
        return found


def wide(row, edge, lanes):
    return jnp.broadcast_to(jnp.concatenate([row] * (lanes // row.shape[1]), axis=1), (edge, lanes))


def choose(fields, index):
    chosen = fields[0]
    for i in range(1, len(fields)):
        chosen = [jnp.where(index == i, new, old) for new, old in zip(fields[i], chosen)]
    return chosen


def slot_rows(info, arrival, slots):
    start = 2 + arrival * slots * 3
    return [info[start + 3 * p : start + 3 * p + 3] for p in range(slots)]


def gather_terms(slots, home, total, tables):
    plane_table, along, inverse = (table[...] for table in tables)
    edge = inverse.shape[0]
    rows = len(slots) * edge
    densities = []
    for moving, index, _ in slots:
        densities.append(spread([m * h for m, h in zip(moving, choose(home, index))]))
    field = jnp.concatenate([density[q] for q in range(4) for density in densities], axis=0)
    field = times_table(field, plane_table)
    field = jnp.concatenate([field[q * rows : (q + 1) * rows] for q in range(4)], axis=1)
    size = along.shape[0] // 2
    along = jnp.concatenate([along[:rows, :rows], along[size : size + rows, :rows]], axis=0)
    field = table_times(along, field)
    field = (field.reshape(len(slots), edge, -1) * inverse[None]).reshape(field.shape)
    field = table_times(along, field)
    lanes = field.shape[1] // 4
    field = jnp.concatenate([field[:, q * lanes : (q + 1) * lanes] for q in range(4)], axis=0)
    field = times_table(field, plane_table)
    for slot, (moving, index, active) in enumerate(slots):
        potential = spread([field[q * rows + slot * edge : q * rows + (slot + 1) * edge] for q in range(4)])
        terms = [active * p * m for p, m in zip(potential, moving)]
        for j in range(len(home)):
            total[j] = [old + jnp.where(index == j, new, 0.0) for old, new in zip(total[j], terms)]


def zero_total(home):
    return [[jnp.zeros_like(q) for q in field] for field in home]


def unfold(fields, table):
    rows = fields[0][0].shape[0]
    lanes = table.shape[0] // 4
    stack = []
    for field in fields:
        for h in (0, 1):
            tiles = [tile_of(q, h) for q in range(4)]
            stack.append(
                jnp.concatenate(
                    [field[t // 2][:, (t % 2) * lanes : (t % 2 + 1) * lanes] for t in tiles], axis=1
                )
            )
    high, low = halves(jnp.concatenate(stack, axis=0))
    plain = dot(high, table) + dot(low, table)
    return [
        jnp.concatenate([plain[k * rows : (k + 1) * rows] for k in (2 * i, 2 * i + 1)], axis=1)
        for i in range(len(fields))
    ]


def slots_of(block, info, near, arrivals, slots, entry):
    edge = block.edge
    fields = [block.quadrants(i) for i in range(block.count)]
    lanes = fields[0][0].shape[1]
    found = []
    for row, far in zip(slot_rows(info, arrivals[0], slots), slot_rows(info, arrivals[1], slots)):
        row = jnp.where(near, row, far)
        own, other, active = (wide(row[e : e + 1], edge, lanes) for e in (entry, 1 - entry, 2))
        found.append((choose(fields, own), other, active))
    return found


def terms_kernel(plan, accumulate, cut, plain, slots, edge, for_travellers, after, *refs):
    outputs = 2 if cut else 1
    refs, outs = refs[:-outputs], refs[-outputs:]
    refs, others = refs[: len(refs) - after], refs[len(refs) - after :]
    blocks = sum(number for number, _ in plan)
    moving, (own, home, *refs) = refs[:blocks], refs[blocks:]
    tables, folding, before = refs[:3], refs[3], refs[4:]
    held = home.shape[0] // (8 * edge)
    count = moving[0].shape[0] // (8 * edge) if for_travellers else moving[0].shape[0]
    own = Fields(own.shape[0] // (8 * edge), edge, own).info()
    near = own[0:1] == (0 if for_travellers else 1)
    home = Fields(held, edge, home)
    home = [home.quadrants(j) for j in range(held)]
    found = []
    for number, arrivals in plan:
        sources, moving = moving[:number], moving[number:]
        if for_travellers:
            block = Fields(count, edge, *sources, near=near)
        else:
            block = PlainFields(count, edge, *sources, near=near[0:1, 0:1], table=folding[...])
        info = block.info() if for_travellers else own
        found += slots_of(block, info, near, arrivals, slots, 0 if for_travellers else 1)
    total = [[before[0][j, q] for q in range(4)] for j in range(held)] if accumulate else zero_total(home)
    group = 2 * slots
    for start in range(0, len(found), group):
        gather_terms(found[start : start + group], home, total, tables)
    if plain:
        for j, field in enumerate(unfold(total, others[0][...])):
            outs[0][j] = field
        return
    if not cut:
        for j, field in enumerate(total):
            for q in range(4):
                outs[0][j, q] = field[q]
        return
    mine, others = outs
    rows = mine.shape[2]
    others[:, 4 * held * rows :, :] = jnp.zeros((others.shape[0], SPARE_ROWS, others.shape[2]), jnp.float32)
    parts = edge // rows
    for k in range(parts):
        group = wide(own[1:2], rows, home[0][0].shape[1]) + k
        group = jnp.where(group >= parts, group - parts, group)
        for j, field in enumerate(total):
            cuts = [[q[p * rows : (p + 1) * rows] for q in field] for p in range(parts)]
            for q, piece in enumerate(choose(cuts, group)):
                if k == 0:
                    mine[j, q] = piece
                else:
                    others[k - 1, (4 * j + q) * rows : (4 * j + q + 1) * rows, :] = piece


def gate_kernel(_, out):
    out[...] = jnp.zeros_like(out)


def sum_kernel(number, *refs):
    parts, (table, terms, trav_out, res_out, trav_total, sems) = refs[:number], refs[number:]
    copies = [pltpu.make_async_copy(terms, res_out, sems.at[0])]
    copies[0].start()
    total = []
    size = parts[0].shape[2]
    for j in range(parts[0].shape[0]):
        starts = [(4 * j + q) * size for q in range(4)]
        total.append([sum((part[k : k + size, :] for part in parts[1:]), parts[0][j, q]) for q, k in enumerate(starts)])
    for j, field in enumerate(unfold(total, table[...])):
        trav_total[j] = field
    copies.append(pltpu.make_async_copy(trav_total, trav_out, sems.at[1]))
    copies[-1].start()
    for copy in copies:
        copy.wait()


VMEM = pl.BlockSpec(memory_space=pltpu.VMEM)
HBM = pl.BlockSpec(memory_space=pl.ANY)
LIMIT = pltpu.CompilerParams(vmem_limit_bytes=32 * 1024 * 1024)
LIMIT_U = pltpu.CompilerParams(vmem_limit_bytes=60 * 1024 * 1024)
LIMIT_W = pltpu.CompilerParams(vmem_limit_bytes=32 * 1024 * 1024)


def cost(microseconds):
    return pl.CostEstimate(flops=int(microseconds * 1e9), bytes_accessed=1024, transcendentals=0)


def from_behind(value, by):
    peers = lax.axis_size("blk")
    return lax.ppermute(value, "blk", [(i, (i + by) % peers) for i in range(peers)])


def other_core(value):
    peers = lax.axis_size("blk")
    return lax.ppermute(value, "blk", [(i, i ^ 1) for i in range(peers)])


def local(residents, travellers, pair_list):
    count, edge, plane = residents.shape
    held = travellers.shape[0]
    steps, slots = pair_list.shape[1:3]
    direct = range(2, steps + 1, 2)
    arrivals = len(direct)
    groups = lax.axis_size("grp")
    part = edge // groups
    fields = 2 * slots
    small = jnp.asarray(small_tables(edge, fields))

    shape = (8 * count * edge + info_rows(steps, slots), plane // 8)
    packed = pl.pallas_call(
        functools.partial(pack_kernel, ("blk", "grp")),
        out_shape=jax.ShapeDtypeStruct(shape, jnp.bfloat16),
        in_specs=[HBM, HBM],
        out_specs=HBM,
        scratch_shapes=[
            pltpu.VMEM(residents.shape, jnp.bfloat16),
            pltpu.SMEM((1, 3, slots, steps), jnp.int32),
            pltpu.VMEM(shape, jnp.bfloat16),
            pltpu.SemaphoreType.DMA((2 + count,)),
        ],
        compiler_params=LIMIT_U,
        cost_estimate=cost(1),
        name="pack",
    )(residents, jnp.transpose(pair_list, (0, 3, 2, 1)))
    *tables, folding, unfolding, moving = pl.pallas_call(
        functools.partial(tables_kernel, fields),
        out_shape=(
            jax.ShapeDtypeStruct((plane // 2, plane // 4), jnp.bfloat16),
            jax.ShapeDtypeStruct((2 * fields * edge, fields * edge), jnp.bfloat16),
            jax.ShapeDtypeStruct((edge, plane), jnp.float32),
            jax.ShapeDtypeStruct((plane // 2, plane // 2), jnp.bfloat16),
            jax.ShapeDtypeStruct((plane // 2, plane // 2), jnp.bfloat16),
            jax.ShapeDtypeStruct((8 * held * edge, plane // 8), jnp.bfloat16),
        ),
        in_specs=[VMEM, VMEM],
        out_specs=(VMEM,) * 6,
        compiler_params=LIMIT,
        cost_estimate=cost(20),
        name="tables",
    )(small, travellers)

    def stage(plan, blocks, home, total, for_travellers, microseconds, name, cut=False, plain=False, after=()):
        number = home[1].shape[0] // (8 * edge)
        if cut:
            out_shape = (
                jax.ShapeDtypeStruct((number, 4, part, plane // 4), jnp.float32),
                jax.ShapeDtypeStruct((groups - 1, number * 4 * part + SPARE_ROWS, plane // 4), jnp.float32),
            )
        elif plain:
            out_shape = jax.ShapeDtypeStruct((number, edge, plane), jnp.float32)
        else:
            out_shape = jax.ShapeDtypeStruct((number, 4, edge, plane // 4), jnp.float32)
        operands = (*blocks, *home, *tables, folding) + (() if total is None else (total,))
        return pl.pallas_call(
            functools.partial(
                terms_kernel, plan, total is not None, cut, plain, slots, edge, for_travellers, len(after)
            ),
            out_shape=out_shape,
            in_specs=[VMEM] * (len(operands) + len(after)),
            out_specs=jax.tree.map(lambda _: VMEM, out_shape),
            compiler_params=LIMIT,
            cost_estimate=cost(microseconds),
            name=name,
        )(*operands, *after)

    last = arrivals - 1

    def straight(k):
        return 1, (2 * k + 1, 2 * k + 1)

    middle = [(1, (2 * k + 2, 2 * k)) for k in range(last)]
    ends = [(2, (0, 2 * last))]

    res_moved = [from_behind(packed, -s) for s in direct]
    res_moved[last], own, moving = lax.optimization_barrier((res_moved[last], packed, moving))
    res_swapped = [other_core(own)] + [other_core(value) for value in res_moved]
    passed, packed_first = lax.optimization_barrier((travellers, packed))
    trav_moved = [from_behind(passed, s) for s in direct]
    trav_swapped = [other_core(passed)]

    def gate(value, microseconds):
        return pl.pallas_call(
            gate_kernel,
            out_shape=jax.ShapeDtypeStruct((8, 128), jnp.float32),
            in_specs=[HBM],
            out_specs=VMEM,
            compiler_params=LIMIT,
            cost_estimate=cost(microseconds),
            name="gate",
        )(value)

    arrived = gate(res_moved[0], 20)

    home = (packed, moving)
    total = stage([straight(last)], [res_moved[last]], home, None, True, 10, "first_traveller_terms")
    blocks = [res_swapped[0], res_swapped[-1]]
    total = stage(ends, blocks, home, total, True, 10, "early_traveller_terms")
    for k in range(last):
        res_moved[k], total = lax.optimization_barrier((res_moved[k], total))
        total = stage([straight(k)], [res_moved[k]], home, total, True, 1, "middle_traveller_terms")
    blocks = [other_core(value) for value in res_moved[:last]]
    mine, others = stage(middle, blocks, home, total, True, 2, "late_traveller_terms", cut=True, after=(arrived,))

    summed = gate(others, 1)
    trav_moved, summed = lax.optimization_barrier((trav_moved, summed))
    trav_swapped += [other_core(value) for value in trav_moved]
    sent = [
        lax.ppermute(others[k - 1], "grp", [(g, (g + k) % groups) for g in range(groups)])
        for k in range(1, groups)
    ]
    home = (packed, packed)
    total = stage(
        [straight(k) for k in range(arrivals)],
        trav_moved,
        home,
        None,
        False,
        0.001,
        "early_resident_terms",
        after=(summed,),
    )
    blocks = [*trav_swapped[1:-1], trav_swapped[0], trav_swapped[-1]]
    res_total = stage(middle + ends, blocks, home, total, False, 0.001, "late_resident_terms", plain=True, after=(unfolding,))
    res_total, sent = lax.optimization_barrier((res_total, sent))
    parts = [mine, *sent]
    trav_total, res_total = pl.pallas_call(
        functools.partial(sum_kernel, len(parts)),
        out_shape=(
            jax.ShapeDtypeStruct((held, part, plane), jnp.float32),
            jax.ShapeDtypeStruct(residents.shape, jnp.float32),
        ),
        in_specs=[VMEM] * (len(parts) + 2),
        out_specs=(HBM, HBM),
        scratch_shapes=[
            pltpu.VMEM((held, part, plane), jnp.float32),
            pltpu.SemaphoreType.DMA((2,)),
        ],
        compiler_params=LIMIT,
        cost_estimate=cost(0.5),
        name="sums",
    )(*parts, unfolding, res_total)
    return res_total, trav_total


def solution(mesh):
    return jax.shard_map(
        local,
        mesh=mesh,
        in_specs=(
            P(("blk", "grp"), None, None),
            P("blk", None, None),
            P(("blk", "grp"), None, None, None),
        ),
        out_specs=(P(("blk", "grp"), None, None), P("blk", "grp", None)),
        check_vma=False,
    )
```
